32 devices in a mesh: dp: 16 (over z, y, x), tensor: 2 (over core).
Axes of the slice: x: 2, y: 2, z: 4, core: 2. Of those that a mesh axis runs over, the one named last changes fastest.
Arguments:
- inputs: bfloat16 [16384, 1024], P('dp'), may hold values from -6 to 6
- first_gain: float32 [1024], replicated, may hold values from 0.25 to 1.75
- query_weight: bfloat16 [1024, 1024], P(None, 'tensor'), may hold values from -0.1875 to 0.1875
- key_matrix: bfloat16 [1024, 512], P(None, 'tensor'), may hold values from -0.1875 to 0.1875
- value_matrix: bfloat16 [1024, 512], P(None, 'tensor'), may hold values from -0.1875 to 0.1875
- query_gain: float32 [64], replicated, may hold values from 0.25 to 1.75
- key_gain: float32 [64], replicated, may hold values from 0.25 to 1.75
- output_weight: bfloat16 [1024, 1024], P('tensor'), may hold values from -0.75 to 0.75
- second_gain: float32 [1024], replicated, may hold values from 0.25 to 1.75
- gate_weight: bfloat16 [1024, 4608], P(None, 'tensor'), may hold values from -0.1875 to 0.1875
- up_weight: bfloat16 [1024, 4608], P(None, 'tensor'), may hold values from -0.1875 to 0.1875
- down_weight: bfloat16 [4608, 1024], P('tensor'), may hold values from -0.09375 to 0.09375
- cotangent: bfloat16 [16384, 1024], P('dp'), may hold values from -6 to 6
Outputs:
- result: bfloat16 [16384, 1024], P('dp')
- input_grad: float32 [16384, 1024], P('dp')
- first_gain_grad: float32 [1024], P('dp')
- query_weight_grad: float32 [1024, 1024], P('dp', 'tensor')
- key_weight_grad: float32 [1024, 512], P('dp', 'tensor')
- value_weight_grad: float32 [1024, 512], P('dp', 'tensor')
- query_gain_grad: float32 [64], replicated
- key_gain_grad: float32 [64], replicated
- output_weight_grad: float32 [1024, 1024], P('tensor', 'dp')
- second_gain_grad: float32 [1024], P('dp')
- gate_weight_grad: float32 [1024, 4608], P('dp', 'tensor')
- up_weight_grad: float32 [1024, 4608], P('dp', 'tensor')
- down_weight_grad: float32 [4608, 1024], P('tensor', 'dp')
The draws below stay inside these ranges and needn't reach their ends.
All inputs are finite; a program needn't handle non-finite values.
Results may differ from the reference program's by a relative error of at most 0.014.
Values sent between devices are 32-bit elements; how exact they have to be, the bound alone decides.
No kernel may reach another device: no remote copies, remote signals or barrier semaphores. Data moves between devices by JAX's collectives and lax.ppermute only.
A program may use at most 192 MiB of HBM per device.

```python
import math
import jax
import jax.numpy as jnp
from jax import lax

MODEL_WIDTH = 1024
QUERY_HEADS = 16
KEY_VALUE_HEADS = 8
HEAD_SIZE = 64
FF = 4608
TOKENS_PER_SHARD = 1024
TOKENS = 16384


def spiked(result, key, source, target, parts, factor):
    def block_of(axis_at):
        return (jnp.arange(result.shape[axis_at]) // (result.shape[axis_at] // parts)).reshape((-1,) + (1,) * (result.ndim - 1 - axis_at))

    first = jax.random.permutation(key, parts)[block_of(target)]
    other_side = (block_of(target) + parts // 2) % parts
    return jnp.where((block_of(source) == first) | (block_of(source) == other_side), factor * result, result)


def level_of(key, dims, shards, smallest, top_value):
    factor_of = 1.0
    for position, blocks in shards:
        heights = jax.random.uniform(jax.random.fold_in(jax.random.fold_in(key, 6), position), (blocks,), jnp.float32, smallest / len(shards), top_value / len(shards))
        factor_of = factor_of * jnp.repeat(jnp.exp(heights), dims[position] // blocks).reshape((-1,) + (1,) * (len(dims) - 1 - position))
    return factor_of


def bell_draw(stream_key, dims, scale, bound, shards=(), held_as=jnp.bfloat16):
    level = level_of(stream_key, dims, shards, -0.22, 0.18) if shards else 1.0
    drawn = jax.random.normal(stream_key, dims, jnp.float32) * scale * level
    return jnp.minimum(jnp.maximum(drawn, -bound), bound).astype(held_as)


def bell_draw_with(stream_key, shape, scale, most, shards, heavy, kind=jnp.bfloat16):
    array = scale * jax.random.normal(stream_key, shape, jnp.float32)
    if shards:
        array = array * level_of(stream_key, shape, shards, -0.22, 0.18)
    return jnp.clip(spiked(array, jax.random.fold_in(stream_key, 3), *heavy), -most, most).astype(kind)


def setup_inputs(seed: int = 0) -> dict:
    seeds = jax.random.split(jax.random.key(seed), 14)
    return {
        "inputs": bell_draw_with(seeds[0], (TOKENS, MODEL_WIDTH), 1.0, 6.0, ((0, 16),), (0, 1, 16, 2.0)),
        "first_gain": jnp.clip(1.0 + 0.15 * jax.random.normal(seeds[1], (MODEL_WIDTH,), jnp.float32), 0.25, 1.75),
        "query_weight": bell_draw(seeds[2], (MODEL_WIDTH, QUERY_HEADS * HEAD_SIZE), MODEL_WIDTH ** -0.5, 0.1875, ((1, 2),)),
        "key_matrix": bell_draw(seeds[3], (MODEL_WIDTH, KEY_VALUE_HEADS * HEAD_SIZE), MODEL_WIDTH ** -0.5, 0.1875, ((1, 2),)),
        "value_matrix": bell_draw(seeds[4], (MODEL_WIDTH, KEY_VALUE_HEADS * HEAD_SIZE), MODEL_WIDTH ** -0.5, 0.1875, ((1, 2),)),
        "query_gain": jnp.clip(1.0 + 0.15 * jax.random.normal(seeds[5], (HEAD_SIZE,), jnp.float32), 0.25, 1.75),
        "key_gain": jnp.clip(1.0 + 0.15 * jax.random.normal(seeds[6], (HEAD_SIZE,), jnp.float32), 0.25, 1.75),
        "output_weight": bell_draw(seeds[7], (QUERY_HEADS * HEAD_SIZE, MODEL_WIDTH), (QUERY_HEADS * HEAD_SIZE // 16) ** -0.5, 0.75, ((0, 2),)),
        "second_gain": jnp.clip(1.0 + 0.15 * jax.random.normal(seeds[8], (MODEL_WIDTH,), jnp.float32), 0.25, 1.75),
        "gate_weight": bell_draw(seeds[9], (MODEL_WIDTH, FF), MODEL_WIDTH ** -0.5, 0.1875, ((1, 2),)),
        "up_weight": bell_draw(seeds[10], (MODEL_WIDTH, FF), MODEL_WIDTH ** -0.5, 0.1875, ((1, 2),)),
        "down_weight": bell_draw(seeds[11], (FF, MODEL_WIDTH), FF ** -0.5, 0.09375, ((0, 2),)),
        "cotangent": bell_draw_with(seeds[12], (TOKENS, MODEL_WIDTH), 1.0, 6.0, ((0, 16),), (0, 1, 16, 2.0)),
    }


EPSILON = 1e-05
ROPE_BASE = 1000000.0
MASKED = -1e+30

@jax.custom_vjp
def to_reduced(v):
    return lax.optimization_barrier(v.astype(jnp.bfloat16)).astype(jnp.float32)

@jax.custom_vjp
def reduced_backward(v):
    return v

def low_keep(v):
    return (to_reduced(v), None)

def low_pass(kept, grad):
    return (grad,)

def back_keep(v):
    return (v, None)

def back_low(kept, grad):
    return (to_reduced(grad),)
to_reduced.defvjp(low_keep, low_pass)
reduced_backward.defvjp(back_keep, back_low)

def exact_product(left_side, right_side):
    return jnp.dot(left_side, right_side, precision=lax.Precision.HIGHEST, preferred_element_type=jnp.float32)

def rms_scale(values, gain):
    return values * lax.rsqrt(lax.optimization_barrier(jnp.mean(values * values, axis=-1, keepdims=True)) + EPSILON) * gain

def rope_tables(length, width):
    half_width = width // 2
    frequency = jnp.exp(jnp.arange(half_width, dtype=jnp.float32) * (-2.0 * math.log(ROPE_BASE) / width))
    angles = jnp.arange(length, dtype=jnp.float32)[:, None] * frequency[None, :]
    angles = jnp.concatenate([angles, angles], axis=1)
    return (jnp.cos(angles)[:, None, :], jnp.sin(angles)[:, None, :])

def rotate(values, cosine_table, sine_table):
    half_width = values.shape[-1] // 2
    turned = jnp.concatenate([-values[..., half_width:], values[..., :half_width]], axis=-1)
    return values * cosine_table + turned * sine_table

def swiglu(gate_in, up_in):
    return jax.nn.silu(gate_in) * up_in

def attend_one(sequence):
    reduced_query, key_low, reduced_value = sequence
    length = reduced_query.shape[0]
    scores = jnp.einsum('qgrd,kgd->grqk', reduced_query, key_low, precision=lax.Precision.HIGHEST) * HEAD_SIZE ** (-0.5)
    scores = reduced_backward(scores)
    causal = jnp.arange(length)[:, None] >= jnp.arange(length)[None, :]
    scores = jnp.where(causal, scores, MASKED)
    probabilities = to_reduced(jax.nn.softmax(scores, axis=-1))
    return jnp.einsum('grqk,kgd->qgrd', probabilities, reduced_value, precision=lax.Precision.HIGHEST)

def forward(inputs, first_gain, query_weight, key_matrix, value_matrix, query_gain, key_gain, output_weight, second_gain, gate_weight, up_weight, down_weight):
    sequence_batch = inputs.shape[0] // TOKENS_PER_SHARD
    cosine_table, sine_table = rope_tables(TOKENS_PER_SHARD, HEAD_SIZE)
    normalized_input = to_reduced(rms_scale(inputs, first_gain))
    query_proj = reduced_backward(exact_product(normalized_input, query_weight)).reshape(sequence_batch, TOKENS_PER_SHARD, QUERY_HEADS, HEAD_SIZE)
    projected_key = reduced_backward(exact_product(normalized_input, key_matrix)).reshape(sequence_batch, TOKENS_PER_SHARD, KEY_VALUE_HEADS, HEAD_SIZE)
    reduced_value = to_reduced(reduced_backward(exact_product(normalized_input, value_matrix))).reshape(sequence_batch, TOKENS_PER_SHARD, KEY_VALUE_HEADS, HEAD_SIZE)
    reduced_query = to_reduced(rotate(rms_scale(query_proj, query_gain), cosine_table, sine_table))
    reduced_query = reduced_query.reshape(sequence_batch, TOKENS_PER_SHARD, KEY_VALUE_HEADS, QUERY_HEADS // KEY_VALUE_HEADS, HEAD_SIZE)
    key_low = to_reduced(rotate(rms_scale(projected_key, key_gain), cosine_table, sine_table))
    mixed = lax.map(jax.checkpoint(attend_one), (reduced_query, key_low, reduced_value))
    mixed = to_reduced(reduced_backward(mixed.reshape(sequence_batch * TOKENS_PER_SHARD, QUERY_HEADS * HEAD_SIZE)))
    middle = inputs + reduced_backward(exact_product(mixed, output_weight))
    normed_mid = to_reduced(rms_scale(middle, second_gain))
    gate_act = reduced_backward(exact_product(normed_mid, gate_weight))
    up_act = reduced_backward(exact_product(normed_mid, up_weight))
    hidden = to_reduced(swiglu(gate_act, up_act))
    return middle + reduced_backward(exact_product(hidden, down_weight))

def reference(inputs, first_gain, query_weight, key_matrix, value_matrix, query_gain, key_gain, output_weight, second_gain, gate_weight, up_weight, down_weight, cotangent):
    floats = tuple((argument.astype(jnp.float32) for argument in (inputs, first_gain, query_weight, key_matrix, value_matrix, query_gain, key_gain, output_weight, second_gain, gate_weight, up_weight, down_weight)))
    output, pullback = jax.vjp(forward, *floats)
    grads = pullback(cotangent.astype(jnp.float32))
    return (output.astype(jnp.bfloat16), grads[0], grads[1], grads[2], grads[3], grads[4], grads[5], grads[6], grads[7], grads[8], grads[9], grads[10], grads[11])
```

```python
import functools
import math

import jax
import jax.numpy as jnp
from jax import lax
from jax.experimental import pallas as pl
from jax.experimental.pallas import tpu as pltpu
from jax.sharding import Mesh, PartitionSpec as P

EPSILON = 1e-05
ROPE_BASE = 1000000.0
BLOCK = 256
VMEM_LIMIT = 60 * 1024 * 1024
SWAP = [(0, 1), (1, 0)]
SHIFT = 8.0


def rms_scale(values, gain):
    return values * lax.rsqrt(jnp.mean(values * values, axis=-1, keepdims=True) + EPSILON) * gain


def rope_tables(length, width):
    half_width = width // 2
    frequency = jnp.exp(
        jnp.arange(half_width, dtype=jnp.float32) * (-2.0 * math.log(ROPE_BASE) / width)
    )
    angles = jnp.arange(length, dtype=jnp.float32)[None, :] * frequency[:, None]
    angles = jnp.concatenate([angles, angles], axis=0)
    return jnp.cos(angles), jnp.sin(angles)


def head_forward(values, gain, cosine, sine):
    scale = lax.rsqrt(jnp.mean(values * values, axis=0, keepdims=True) + EPSILON)
    normed = values * scale * gain
    half_width = values.shape[0] // 2
    turned = jnp.concatenate([-normed[half_width:], normed[:half_width]], axis=0)
    return normed * cosine + turned * sine


def head_backward(values, gain, cosine, sine, grad):
    half_width = values.shape[0] // 2
    crossed = grad * sine
    back = grad * cosine + jnp.concatenate([crossed[half_width:], -crossed[:half_width]], axis=0)
    scale = lax.rsqrt(jnp.mean(values * values, axis=0, keepdims=True) + EPSILON)
    hat = values * scale
    scaled = back * gain
    out = scale * (scaled - hat * jnp.mean(scaled * hat, axis=0, keepdims=True))
    return out, fold_lanes(back * hat)


def fold_lanes(values):
    total = values[:, :128]
    for at in range(128, values.shape[1], 128):
        total = total + values[:, at : at + 128]
    return total


def visible(size):
    key = lax.broadcasted_iota(jnp.int32, (size, size), 0)
    query = lax.broadcasted_iota(jnp.int32, (size, size), 1)
    return key <= query


def dot32(left, right):
    return jnp.dot(left, right, preferred_element_type=jnp.float32)


def attend_kernel(
    query_ref, key_ref, value_ref, query_gain_ref, key_gain_ref, cosine_ref, sine_ref,
    mixed_ref, query_low_ref, key_low_ref, value_low_ref, total_ref,
):
    width, length = key_ref.shape
    repeat = query_ref.shape[0] // width
    score_scale = width ** (-0.5)
    cosine, sine = cosine_ref[...], sine_ref[...]
    key = head_forward(key_ref[...], key_gain_ref[...], cosine, sine)
    key_low_ref[...] = key.astype(jnp.bfloat16)
    key_rows = key.T.astype(jnp.bfloat16)
    value_low = value_ref[...].astype(jnp.bfloat16)
    value_low_ref[...] = value_low
    ones = jnp.ones((16, length), jnp.bfloat16)
    value_and_one = jnp.concatenate([value_low, ones], axis=0)
    mask = visible(BLOCK)
    for head in range(repeat):
        at = slice(head * width, (head + 1) * width)
        query = head_forward(query_ref[at, :], query_gain_ref[...], cosine, sine)
        query_low = (query.astype(jnp.bfloat16).astype(jnp.float32) * score_scale).astype(
            jnp.bfloat16
        )
        query_low_ref[at, :] = query_low
        for start in range(0, length, BLOCK):
            stop = start + BLOCK
            columns = query_low[:, start:stop]
            near = jnp.exp(dot32(key_rows[start:stop], columns))
            near = jnp.where(mask, near, 0.0).astype(jnp.bfloat16)
            out = dot32(value_and_one[:, start:stop], near)
            if start:
                far = jnp.exp(dot32(key_rows[:start], columns)).astype(jnp.bfloat16)
                out = out + dot32(value_and_one[:, :start], far)
            total = out[width : width + 1]
            mixed_ref[at, start:stop] = (out[:width] / total).astype(jnp.bfloat16)
            total_ref[head : head + 1, start:stop] = jnp.log(total)


def attend_back_kernel(
    query_ref, key_ref, query_gain_ref, key_gain_ref, cosine_ref, sine_ref,
    query_low_ref, key_low_ref, value_low_ref, mixed_ref, total_ref, back_ref,
    query_back_ref, key_back_ref, value_back_ref, query_part_ref, key_part_ref,
    key_sum, value_sum,
):
    width, length = key_ref.shape
    repeat = query_ref.shape[0] // width
    score_scale = width ** (-0.5)
    cosine, sine = cosine_ref[...], sine_ref[...]

    def rows_of(value):
        return value.astype(jnp.float32).T.astype(jnp.bfloat16)

    key_low = key_low_ref[...]
    key_rows = rows_of(key_low)
    value_rows = rows_of(value_low_ref[...])
    mask = visible(BLOCK)
    key_sum[...] = jnp.zeros_like(key_sum)
    value_sum[...] = jnp.zeros_like(value_sum)
    query_part = jnp.zeros((width, 128), jnp.float32)
    for head in range(repeat):
        at = slice(head * width, (head + 1) * width)
        query_low = query_low_ref[at, :]
        query_rows = rows_of(query_low)
        back = back_ref[at, :]
        back_rows = rows_of(back)
        delta = jnp.sum(
            mixed_ref[at, :].astype(jnp.float32) * back.astype(jnp.float32), axis=0, keepdims=True
        )
        total = total_ref[head : head + 1, :]
        grads = []
        for start in range(0, length, BLOCK):
            stop = start + BLOCK
            columns, incoming = query_low[:, start:stop], back[:, start:stop]
            shift, inner = total[:, start:stop], delta[:, start:stop]
            grad = None
            for low, high in ((start, stop), (0, start)):
                if low == high:
                    continue
                weights = jnp.exp(dot32(key_rows[low:high], columns) - shift)
                if low == start:
                    weights = jnp.where(mask, weights, 0.0)
                score = weights * (dot32(value_rows[low:high], incoming) - inner)
                score = score.astype(jnp.bfloat16)
                value_sum[low:high] += dot32(weights.astype(jnp.bfloat16), back_rows[start:stop])
                key_sum[low:high] += dot32(score, query_rows[start:stop])
                part = dot32(key_low[:, low:high], score)
                grad = part if grad is None else grad + part
            grads.append(grad * score_scale)
        out, part = head_backward(
            query_ref[at, :], query_gain_ref[...], cosine, sine, jnp.concatenate(grads, axis=1)
        )
        query_back_ref[at, :] = out.astype(jnp.bfloat16)
        query_part = query_part + part
    out, part = head_backward(key_ref[...], key_gain_ref[...], cosine, sine, key_sum[...].T)
    key_back_ref[...] = out.astype(jnp.bfloat16)
    value_back_ref[...] = value_sum[...].T.astype(jnp.bfloat16)
    query_part_ref[...] = query_part
    key_part_ref[...] = part


def group_block(rows, length):
    return pl.BlockSpec((rows, length), lambda group: (group, 0))


def shared_block(rows, length):
    return pl.BlockSpec((rows, length), lambda group: (0, 0))


def attend(query, key, value, query_gain, key_gain, cosine, sine):
    width, length = cosine.shape
    groups = key.shape[0] // width
    wide = query.shape[0] // groups
    low = jnp.bfloat16
    return pl.pallas_call(
        attend_kernel,
        grid=(groups,),
        in_specs=[
            group_block(wide, length),
            group_block(width, length),
            group_block(width, length),
            shared_block(width, 1),
            shared_block(width, 1),
            shared_block(width, length),
            shared_block(width, length),
        ],
        out_specs=[
            group_block(wide, length),
            group_block(wide, length),
            group_block(width, length),
            group_block(width, length),
            group_block(8, length),
        ],
        out_shape=[
            jax.ShapeDtypeStruct(query.shape, low),
            jax.ShapeDtypeStruct(query.shape, low),
            jax.ShapeDtypeStruct(key.shape, low),
            jax.ShapeDtypeStruct(key.shape, low),
            jax.ShapeDtypeStruct((groups * 8, length), jnp.float32),
        ],
        compiler_params=pltpu.CompilerParams(vmem_limit_bytes=VMEM_LIMIT),
        cost_estimate=pl.CostEstimate(
            flops=10**10, bytes_accessed=10**7, transcendentals=query.size * length // width
        ),
        name="attend",
    )(query, key, value, query_gain, key_gain, cosine, sine)


def attend_back(query, key, query_gain, key_gain, cosine, sine, kept, mixed_back):
    mixed, query_low, key_low, value_low, total = kept
    width, length = cosine.shape
    groups = key.shape[0] // width
    wide = query.shape[0] // groups
    low = jnp.bfloat16
    return pl.pallas_call(
        attend_back_kernel,
        grid=(groups,),
        in_specs=[
            group_block(wide, length),
            group_block(width, length),
            shared_block(width, 1),
            shared_block(width, 1),
            shared_block(width, length),
            shared_block(width, length),
            group_block(wide, length),
            group_block(width, length),
            group_block(width, length),
            group_block(wide, length),
            group_block(8, length),
            group_block(wide, length),
        ],
        out_specs=[
            group_block(wide, length),
            group_block(width, length),
            group_block(width, length),
            group_block(width, 128),
            group_block(width, 128),
        ],
        out_shape=[
            jax.ShapeDtypeStruct(query.shape, low),
            jax.ShapeDtypeStruct(key.shape, low),
            jax.ShapeDtypeStruct(key.shape, low),
            jax.ShapeDtypeStruct((groups * width, 128), jnp.float32),
            jax.ShapeDtypeStruct((groups * width, 128), jnp.float32),
        ],
        scratch_shapes=[
            pltpu.VMEM((length, width), jnp.float32),
            pltpu.VMEM((length, width), jnp.float32),
        ],
        compiler_params=pltpu.CompilerParams(vmem_limit_bytes=VMEM_LIMIT),
        cost_estimate=pl.CostEstimate(
            flops=2 * 10**10, bytes_accessed=10**7, transcendentals=query.size * length // width
        ),
        name="attend_back",
    )(query, key, query_gain, key_gain, cosine, sine, query_low, key_low, value_low, mixed, total,
      mixed_back)


def cols_dot(left, right):
    return lax.dot_general(
        left, right, (((1,), (1,)), ((), ())), preferred_element_type=jnp.float32
    )


def units_kernel(sums, *refs):
    _, normed_ref, incoming_ref, gate_ref, up_ref, down_ref, *refs = refs
    hidden_ref, gate_back_ref, up_back_ref = refs[-5:-2] if sums else refs
    rows = normed_ref.shape[0]
    gate_weight, up_weight, down_weight = gate_ref[...], up_ref[...], down_ref[...]
    if sums:
        mid_ref, branch_ref = refs[-2:]

        @pl.when(pl.program_id(0) == 0)
        def _():
            if sums == 2:
                mid_ref[...], branch_ref[...] = refs[0][...], refs[1][...]
            else:
                mid_ref[...] = jnp.zeros_like(mid_ref)
                branch_ref[...] = jnp.zeros_like(branch_ref)

    for start in range(0, rows, BLOCK):
        at = slice(start, start + BLOCK)
        normed, incoming = normed_ref[at, :], incoming_ref[at, :]
        gate_act = dot32(normed, gate_weight)
        up_act = dot32(normed, up_weight)
        hidden_back = cols_dot(incoming, down_weight)
        sigmoid = 1.0 / (1.0 + jnp.exp(-gate_act))
        silu = gate_act * sigmoid
        hidden = (silu * up_act).astype(jnp.bfloat16)
        gate_in = (hidden_back * up_act * (sigmoid + silu * (1.0 - sigmoid))).astype(jnp.bfloat16)
        up_in = (hidden_back * silu).astype(jnp.bfloat16)
        hidden_ref[at, :] = hidden
        gate_back_ref[at, :] = gate_in
        up_back_ref[at, :] = up_in
        if sums:
            mid_ref[at, :] += cols_dot(gate_in, gate_weight) + cols_dot(up_in, up_weight)
            branch_ref[at, :] += dot32(hidden, down_weight)


def units_call(normed, incoming, gate_weight, up_weight, down_weight, first, count, sums, start=()):
    rows, width = normed.shape
    tile = BLOCK if count % BLOCK == 0 else BLOCK // 2
    low = jnp.bfloat16
    whole = pl.BlockSpec((rows, width), lambda at, base: (0, 0), pipeline_mode=pl.Buffered(1))
    by_unit = pl.BlockSpec((width, tile), lambda at, base: (0, base[0] + at))
    out_tile = pl.BlockSpec((rows, tile), lambda at, base: (0, at))
    out_shape = [jax.ShapeDtypeStruct((rows, count), low)] * 3
    out_specs = [out_tile] * 3
    if sums:
        out_shape = out_shape + [jax.ShapeDtypeStruct((rows, width), jnp.float32)] * 2
        out_specs = out_specs + [pl.BlockSpec((rows, width), lambda at, base: (0, 0))] * 2
    base = jnp.asarray(first // tile, jnp.int32).reshape(1)
    return pl.pallas_call(
        functools.partial(units_kernel, sums),
        grid_spec=pltpu.PrefetchScalarGridSpec(
            num_scalar_prefetch=1,
            grid=(count // tile,),
            in_specs=[
                whole,
                whole,
                by_unit,
                by_unit,
                pl.BlockSpec((tile, width), lambda at, base: (base[0] + at, 0)),
            ]
            + [whole] * len(start),
            out_specs=out_specs,
        ),
        out_shape=out_shape,
        compiler_params=pltpu.CompilerParams(vmem_limit_bytes=VMEM_LIMIT),
        cost_estimate=pl.CostEstimate(
            flops=2 * rows * width * count * (6 if sums else 3),
            bytes_accessed=10**7,
            transcendentals=rows * count,
        ),
        name="units",
    )(base, normed, incoming, gate_weight, up_weight, down_weight, *start)


def contract_cols(left_side, right_side):
    return lax.dot_general(
        left_side, right_side, (((1,), (1,)), ((), ())), preferred_element_type=jnp.float32
    )


def contract_rows(left_side, right_side):
    return lax.dot_general(
        left_side, right_side, (((0,), (0,)), ((), ())), preferred_element_type=jnp.float32
    )


def back_product(left_side, right_side):
    return lax.dot_general(
        left_side, right_side, (((0,), (1,)), ((), ())), preferred_element_type=jnp.float32
    )


def product(left_side, right_side):
    return jnp.dot(left_side, right_side, preferred_element_type=jnp.float32)


def swap(value, axis):
    return lax.ppermute(value, axis, SWAP)


def core_sum(value):
    return value + swap(value, "tensor")


def core_sum_halves(make, rows):
    half = rows // 2
    first, second = make(0, half), make(half, rows)
    return jnp.concatenate([core_sum(first), core_sum(second)], axis=0)


def tie(*values):
    return lax.optimization_barrier(values)


def line_exchange(kept, length):
    own = kept.shape[0] // length
    blocks = [kept[at * own : (at + 1) * own] for at in range(length)]
    arrived = [
        lax.ppermute(
            blocks[away], "line", [(at, (at + away) % length) for at in range(length)]
        )
        for away in range(1, length)
    ]
    return blocks[0], arrived


def line_sum(own, arrived):
    for part in arrived:
        own = own + part
    return own


def pair_sums(own, arrived):
    mine, other = own, None
    for away, part in enumerate(arrived, 1):
        if away % 2 == 0:
            mine = mine + part
        else:
            other = part if other is None else other + part
    return mine, other


def in_order(half, mine, other):
    return jnp.concatenate(
        [jnp.where(half == 0, mine, other), jnp.where(half == 0, other, mine)], axis=1
    )


class Plane:
    def __init__(self, pieces):
        self.pieces = pieces

    @staticmethod
    def rows(left, start, stop):
        quarter = left.shape[0] // 4
        return left[start * quarter : stop * quarter]

    def products(self, for_near, for_mid):
        return [
            (contract_cols if transposed else product)(
                for_near(left) if near_first else for_mid(left), right
            )
            for left, right, near_first, transposed in self.pieces
        ]

    def send(self):
        return self.products(
            lambda left: self.rows(left, 0, 2),
            lambda left: jnp.concatenate([self.rows(left, 0, 1), self.rows(left, 2, 3)], axis=0),
        )

    def go(self, out):
        return [
            swap(part, "near" if piece[2] else "mid") for part, piece in zip(out, self.pieces)
        ]

    def follow(self, got):
        parts = self.products(lambda left: self.rows(left, 2, 3), lambda left: self.rows(left, 1, 2))
        return [part + late[: part.shape[0]] for part, late in zip(parts, got)]

    def pass_on(self, out):
        return [
            swap(part, "mid" if piece[2] else "near") for part, piece in zip(out, self.pieces)
        ]

    def keep(self, got, passed):
        def own(left):
            return self.rows(left, 3, 4)

        parts = self.products(own, own)
        return jnp.concatenate(
            [
                part + early[part.shape[0] :] + late
                for part, early, late in zip(parts, got, passed)
            ],
            axis=1,
        )


class Owners:
    def __init__(self, width):
        self.length = lax.axis_size("line")
        self.width = width
        self.own = width // (4 * self.length)
        line, mid, near = (lax.axis_index(name) for name in ("line", "mid", "near"))
        place = lax.broadcasted_iota(jnp.int32, (2, 2, self.length, self.own, 1), 0)
        row = lax.broadcasted_iota(jnp.int32, place.shape, 1)
        distance = lax.broadcasted_iota(jnp.int32, place.shape, 2)
        entry = lax.broadcasted_iota(jnp.int32, place.shape, 3)
        owner_near = (place + near + 1) % 2
        owner_mid = (row + mid + 1) % 2
        owner_line = (distance + line) % self.length
        feature = ((owner_line * 2 + owner_mid) * 2 + owner_near) * self.own + entry
        self.feature = feature

    def select(self, order):
        column = lax.broadcasted_iota(jnp.int32, (1, self.width), 1)
        feature = self.feature.transpose(order + (3, 4)).reshape(self.width, 1)
        return (feature == column).astype(jnp.bfloat16)

    def plane_first(self, left):
        return contract_cols(self.select((0, 1, 2)), left).astype(jnp.bfloat16)

    def line_first(self, left):
        return contract_cols(self.select((2, 0, 1)), left).astype(jnp.bfloat16)


def line_everywhere(value):
    length = lax.axis_size("line")
    found = [value] + [
        lax.ppermute(value, "line", [(at, (at + away) % length) for at in range(length)])
        for away in range(1, length)
    ]
    return found


def in_line_order(found):
    length = len(found)
    stacked = jnp.stack(found)
    total = jnp.zeros_like(found[0])
    for at in range(length):
        away = (lax.axis_index("line") - at) % length
        total = total + lax.dynamic_index_in_dim(stacked, away, 0, keepdims=False)
    return total


def local(
    inputs,
    first_gain,
    query_weight,
    key_matrix,
    value_matrix,
    query_gain,
    key_gain,
    output_weight,
    second_gain,
    gate_weight,
    up_weight,
    down_weight,
    cotangent,
):
    row_count, model_width = inputs.shape
    head_dim = query_gain.shape[0]
    units = gate_weight.shape[1]
    cosine_table, sine_table = rope_tables(row_count, head_dim)
    owners = Owners(model_width)
    length = owners.length

    core = lax.axis_index("tensor")
    half = lax.axis_index("line") % 2
    partners = [(at, at + 1 - 2 * (at % 2)) for at in range(length)]
    core_rows = row_count // 2

    def my_rows(value):
        return lax.dynamic_slice_in_dim(value, core * core_rows, core_rows, axis=0)

    def to_partner(value):
        return lax.ppermute(value, "line", partners)

    cotangent_mine = my_rows(cotangent).astype(jnp.float32) * SHIFT
    early = core_rows // 2
    far_first = to_partner(cotangent_mine[:early])
    source = inputs.astype(jnp.float32)
    first_normed, first_pull = jax.vjp(rms_scale, source, first_gain)
    normalized_input = first_normed.astype(jnp.bfloat16)

    def project(weight):
        return lax.dot_general(
            weight,
            normalized_input,
            (((0,), (1,)), ((), ())),
            preferred_element_type=jnp.float32,
        )

    query_proj, projected_key = project(query_weight), project(key_matrix)
    gains = (query_gain[:, None], key_gain[:, None])
    kept = attend(
        query_proj, projected_key, project(value_matrix), *gains, cosine_table, sine_table
    )
    *kept, far_first, cotangent_mine = tie(*kept, far_first, cotangent_mine)
    mixed = kept[0]
    far_second = to_partner(cotangent_mine[early:])
    attention = core_sum_halves(
        lambda a, b: contract_rows(mixed[:, a:b], output_weight), row_count
    )
    middle = source + attention
    second_normed, second_pull = jax.vjp(rms_scale, middle, second_gain)
    normed_mid = second_normed.astype(jnp.bfloat16)
    hat = middle * lax.rsqrt(jnp.mean(middle * middle, axis=-1, keepdims=True) + EPSILON)
    hat, normed_mid, far_second = tie(hat, normed_mid, far_second)
    hat_far = to_partner(my_rows(hat))
    cotangent_far = jnp.concatenate([far_first, far_second], axis=0)

    weights = (gate_weight, up_weight, down_weight)

    alone = units * 2 // 9 // 256 * 256
    paired = (units - alone) // 2
    hidden_1, gate_1, up_1, *sums_1 = units_call(normed_mid, cotangent, *weights, 0, alone, 1)
    normed_left = owners.plane_first(normed_mid)
    cotangent_left = owners.plane_first(cotangent)
    up_cut = alone // 256 * 128
    plane_1 = Plane(
        [
            (cotangent_left, hidden_1, True, False),
            (normed_left, gate_1, False, False),
            (normed_left, up_1[:, :up_cut], True, False),
            (normed_left, up_1[:, up_cut:], False, False),
        ]
    )
    sent_1 = plane_1.send()
    cotangent_swapped = swap(cotangent_far, "tensor")
    sent_1, normed_mid, cotangent_swapped = tie(sent_1, normed_mid, cotangent_swapped)
    got_1 = plane_1.go(sent_1)
    hidden_2, gate_2, up_2, mid_part, branch_part = units_call(
        normed_mid, cotangent, *weights, alone, units - alone, 2, sums_1
    )
    got_1, mid_part, hat_far, cotangent_swapped = tie(got_1, mid_part, hat_far, cotangent_swapped)

    hat_swapped = swap(hat_far, "tensor")
    follow_1 = plane_1.follow(got_1)
    far_cotangent = jnp.concatenate([cotangent_far, cotangent_swapped], axis=0) * (1.0 / SHIFT)
    far_cotangent = far_cotangent.astype(jnp.bfloat16)
    follow_1, hat_far, hat_swapped, far_cotangent, mid_part = tie(
        follow_1, hat_far, hat_swapped, far_cotangent, mid_part
    )
    passed_1 = plane_1.pass_on(follow_1)
    mid_swapped = swap(mid_part, "tensor")
    far_normed = (jnp.concatenate([hat_far, hat_swapped], axis=0) * second_gain).astype(
        jnp.bfloat16
    )

    def my_half(array, start, axis):
        return lax.dynamic_slice_in_dim(array, start + half * paired, paired, axis=axis)

    far_hidden, far_gate, far_up = units_call(
        far_normed, far_cotangent, *weights, alone + half * paired, paired, 0
    )
    passed_1, far_hidden, far_gate, far_up, mid_swapped = tie(
        passed_1, far_hidden, far_gate, far_up, mid_swapped
    )
    normed_both = jnp.concatenate([normed_left, owners.plane_first(far_normed)], axis=1)
    cotangent_both = jnp.concatenate([cotangent_left, owners.plane_first(far_cotangent)], axis=1)
    hidden_both = jnp.concatenate([my_half(hidden_2, 0, 1), far_hidden], axis=0)
    gate_both = jnp.concatenate([my_half(gate_2, 0, 1), far_gate], axis=0)
    plane_2 = Plane(
        [(cotangent_both, hidden_both, True, False), (normed_both, gate_both, False, False)]
    )
    sent_2 = plane_2.send()
    sent_2, passed_1, mid_swapped = tie(sent_2, passed_1, mid_swapped)
    got_2 = plane_2.go(sent_2)
    line_1 = line_exchange(plane_1.keep(got_1, passed_1), length)
    mid_back = mid_part + mid_swapped
    middle_norm_back, second_gain_grad = second_pull(mid_back)
    middle_grad = cotangent.astype(jnp.float32) + middle_norm_back
    attention_back = middle_grad.astype(jnp.bfloat16)
    mixed_back = contract_cols(output_weight, attention_back).astype(jnp.bfloat16)
    query_back, key_back, value_back, query_part, key_part = attend_back(
        query_proj, projected_key, *gains, cosine_table, sine_table, kept, mixed_back
    )
    got_2, line_1, query_back, key_back, value_back, attention_back = tie(
        got_2, line_1, query_back, key_back, value_back, attention_back
    )
    follow_2 = plane_2.follow(got_2)
    follow_2, attention_back = tie(follow_2, attention_back)
    passed_2 = plane_2.pass_on(follow_2)
    up_both = jnp.concatenate([my_half(up_2, 0, 1), far_up], axis=0)
    plane_3 = Plane(
        [
            (normed_both, up_both, True, False),
            (owners.plane_first(attention_back), mixed, False, True),
        ]
    )
    sent_3 = plane_3.send()
    normed_part = (
        back_product(query_back, query_weight)
        + back_product(key_back, key_matrix)
        + back_product(value_back, value_matrix)
    )
    passed_2, sent_3, normed_part = tie(passed_2, sent_3, normed_part)
    got_3 = plane_3.go(sent_3)
    line_2 = line_exchange(plane_2.keep(got_2, passed_2), length)
    input_left = owners.plane_first(normalized_input)
    plane_4 = Plane(
        [
            (input_left, jnp.concatenate([key_back, value_back], axis=0), True, True),
            (input_left, query_back, False, True),
        ]
    )
    sent_4 = plane_4.send()
    got_3, line_2, sent_4, normed_part = tie(got_3, line_2, sent_4, normed_part)
    follow_3 = plane_3.follow(got_3)
    follow_3, normed_part, branch_part = tie(follow_3, normed_part, branch_part)
    passed_3 = plane_3.pass_on(follow_3)
    normed_back = core_sum(normed_part)
    source_back, first_gain_grad = first_pull(normed_back)
    input_grad = middle_grad + source_back
    passed_3, sent_4, input_grad, first_gain_grad = tie(
        passed_3, sent_4, input_grad, first_gain_grad
    )
    got_4 = plane_4.go(sent_4)
    line_3 = line_exchange(plane_3.keep(got_3, passed_3), length)
    head_gains = jnp.concatenate(
        [jnp.sum(part.reshape(-1, head_dim, 128), axis=(0, 2)) for part in (query_part, key_part)]
    )
    got_4, line_3, head_gains = tie(got_4, line_3, head_gains)
    follow_4 = plane_4.follow(got_4)
    rows = jnp.stack(
        [
            first_gain_grad,
            second_gain_grad,
            jnp.pad(core_sum(head_gains), (0, model_width - 2 * head_dim)),
        ]
    )
    rows = jnp.pad(rows, ((0, 5), (0, 0)))
    follow_4, rows = tie(follow_4, rows)
    passed_4 = plane_4.pass_on(follow_4)
    branch = core_sum(branch_part)
    result = (middle + branch).astype(jnp.bfloat16)
    rows = rows + swap(rows, "near")
    rows = rows + swap(rows, "mid")
    passed_4, rows, result = tie(passed_4, rows, result)
    line_4 = line_exchange(plane_4.keep(got_4, passed_4), length)
    rows = in_line_order(line_everywhere(rows))
    attention_shard = line_sum(*line_4)

    def split(total, count):
        return [total[:, at : at + count] for at in range(0, total.shape[1], count)]

    halves = [split(side, paired) for side in pair_sums(*line_2)]
    sides = [side[:, :paired] for side in pair_sums(*line_3)]
    down_2, gate_2, up_2 = (
        in_order(half, mine, other)
        for mine, other in zip(halves[0] + sides[:1], halves[1] + sides[1:])
    )
    first = line_sum(*line_1)
    down_1, gate_1, up_1 = first[:, :alone], first[:, alone : 2 * alone], first[:, 2 * alone :]
    down_shard, gate_shard, up_shard = (
        jnp.concatenate(pair, axis=1)
        for pair in ((down_1, down_2), (gate_1, gate_2), (up_1, up_2))
    )
    output_shard = line_sum(line_3[0][:, paired:], [part[:, paired:] for part in line_3[1]])
    key_cut = key_back.shape[0]
    pair_cut = 2 * key_cut
    index = (lax.axis_index("line") * 2 + lax.axis_index("mid")) * 2 + lax.axis_index("near")
    gains = lax.dynamic_slice(rows, (0, index * owners.own), (2, owners.own))
    return (
        result,
        input_grad,
        gains[0],
        attention_shard[:, pair_cut:],
        attention_shard[:, :key_cut],
        attention_shard[:, key_cut:pair_cut],
        rows[2, :head_dim],
        rows[2, head_dim : 2 * head_dim],
        output_shard.T,
        gains[1],
        gate_shard,
        up_shard,
        down_shard.T,
    )


def solution(mesh):
    line = mesh.shape["dp"] // 4
    shaped = Mesh(
        mesh.devices.reshape(line, 2, 2, mesh.shape["tensor"]), ("line", "mid", "near", "tensor")
    )
    dp = ("line", "mid", "near")
    placed = (
        P(dp, None),
        P(),
        P(None, "tensor"),
        P(None, "tensor"),
        P(None, "tensor"),
        P(),
        P(),
        P("tensor", None),
        P(),
        P(None, "tensor"),
        P(None, "tensor"),
        P("tensor", None),
        P(dp, None),
    )
    return jax.shard_map(
        local,
        mesh=shaped,
        in_specs=placed,
        out_specs=(
            P(dp, None),
            P(dp, None),
            P(dp),
            P(dp, "tensor"),
            P(dp, "tensor"),
            P(dp, "tensor"),
            P(),
            P(),
            P("tensor", dp),
            P(dp),
            P(dp, "tensor"),
            P(dp, "tensor"),
            P("tensor", dp),
        ),
        check_vma=False,
    )
```

```python
import functools
import math

import jax
import jax.numpy as jnp
import numpy as np
from jax import lax
from jax.experimental import pallas as pl
from jax.experimental.pallas import tpu as pltpu
from jax.sharding import Mesh, PartitionSpec as P

EPSILON = 1e-05
ROPE_BASE = 1000000.0
BLOCK = 256
SMALL_COST = pl.CostEstimate(flops=10**8, bytes_accessed=10**6, transcendentals=0)
VMEM_LIMIT = 60 * 1024 * 1024
SWAP = [(0, 1), (1, 0)]
SHIFT = 8.0


def rms_scale(values, gain):
    return values * lax.rsqrt(jnp.mean(values * values, axis=-1, keepdims=True) + EPSILON) * gain


def rope_tables(length, width):
    half_width = width // 2
    frequency = np.exp(
        np.arange(half_width, dtype=np.float32) * np.float32(-2.0 * math.log(ROPE_BASE) / width)
    )
    angles = np.arange(length, dtype=np.float32)[None, :] * frequency[:, None]
    angles = np.concatenate([angles, angles], axis=0)
    return jnp.asarray(np.cos(angles)), jnp.asarray(np.sin(angles))


def head_forward(values, gain, cosine, sine):
    scale = lax.rsqrt(jnp.mean(values * values, axis=0, keepdims=True) + EPSILON)
    normed = values * scale * gain
    half_width = values.shape[0] // 2
    turned = jnp.concatenate([-normed[half_width:], normed[:half_width]], axis=0)
    return normed * cosine + turned * sine


def head_backward(values, gain, cosine, sine, grad):
    half_width = values.shape[0] // 2
    crossed = grad * sine
    back = grad * cosine + jnp.concatenate([crossed[half_width:], -crossed[:half_width]], axis=0)
    scale = lax.rsqrt(jnp.mean(values * values, axis=0, keepdims=True) + EPSILON)
    hat = values * scale
    scaled = back * gain
    out = scale * (scaled - hat * jnp.mean(scaled * hat, axis=0, keepdims=True))
    return out, fold_lanes(back * hat)


def fold_lanes(values):
    total = values[:, :128]
    for at in range(128, values.shape[1], 128):
        total = total + values[:, at : at + 128]
    return total


def visible(size):
    key = lax.broadcasted_iota(jnp.int32, (size, size), 0)
    query = lax.broadcasted_iota(jnp.int32, (size, size), 1)
    return key <= query


def dot32(left, right):
    return jnp.dot(left, right, preferred_element_type=jnp.float32)


def attend_kernel(
    query_ref, key_ref, value_ref, query_gain_ref, key_gain_ref, cosine_ref, sine_ref,
    mixed_ref, query_low_ref, key_low_ref, value_low_ref, total_ref,
):
    width, length = key_ref.shape
    repeat = query_ref.shape[0] // width
    score_scale = width ** (-0.5)
    cosine, sine = cosine_ref[...], sine_ref[...]
    key = head_forward(key_ref[...], key_gain_ref[...], cosine, sine)
    key_low_ref[...] = key.astype(jnp.bfloat16)
    key_rows = key.T.astype(jnp.bfloat16)
    value_low = value_ref[...].astype(jnp.bfloat16)
    value_low_ref[...] = value_low
    ones = jnp.ones((16, length), jnp.bfloat16)
    value_and_one = jnp.concatenate([value_low, ones], axis=0)
    mask = visible(BLOCK)
    for head in range(repeat):
        at = slice(head * width, (head + 1) * width)
        query = head_forward(query_ref[at, :], query_gain_ref[...], cosine, sine)
        query_low = (query.astype(jnp.bfloat16).astype(jnp.float32) * score_scale).astype(
            jnp.bfloat16
        )
        query_low_ref[at, :] = query_low
        for start in range(0, length, BLOCK):
            stop = start + BLOCK
            columns = query_low[:, start:stop]
            near = jnp.exp(dot32(key_rows[start:stop], columns))
            near = jnp.where(mask, near, 0.0).astype(jnp.bfloat16)
            out = dot32(value_and_one[:, start:stop], near)
            if start:
                far = jnp.exp(dot32(key_rows[:start], columns)).astype(jnp.bfloat16)
                out = out + dot32(value_and_one[:, :start], far)
            total = out[width : width + 1]
            mixed_ref[at, start:stop] = (out[:width] / total).astype(jnp.bfloat16)
            total_ref[head : head + 1, start:stop] = jnp.log(total)


def attend_back_kernel(
    query_ref, key_ref, query_gain_ref, key_gain_ref, cosine_ref, sine_ref,
    query_low_ref, key_low_ref, value_low_ref, mixed_ref, total_ref, back_ref,
    query_back_ref, key_back_ref, value_back_ref, query_part_ref, key_part_ref,
    key_sum, value_sum,
):
    width, length = key_ref.shape
    repeat = query_ref.shape[0] // width
    score_scale = width ** (-0.5)
    cosine, sine = cosine_ref[...], sine_ref[...]

    def rows_of(value):
        return value.astype(jnp.float32).T.astype(jnp.bfloat16)

    key_low = key_low_ref[...]
    key_rows = rows_of(key_low)
    value_rows = rows_of(value_low_ref[...])
    mask = visible(BLOCK)
    key_sum[...] = jnp.zeros_like(key_sum)
    value_sum[...] = jnp.zeros_like(value_sum)
    query_part = jnp.zeros((width, 128), jnp.float32)
    for head in range(repeat):
        at = slice(head * width, (head + 1) * width)
        query_low = query_low_ref[at, :]
        query_rows = rows_of(query_low)
        back = back_ref[at, :]
        back_rows = rows_of(back)
        delta = jnp.sum(
            mixed_ref[at, :].astype(jnp.float32) * back.astype(jnp.float32), axis=0, keepdims=True
        )
        total = total_ref[head : head + 1, :]
        grads = []
        for start in range(0, length, BLOCK):
            stop = start + BLOCK
            columns, incoming = query_low[:, start:stop], back[:, start:stop]
            shift, inner = total[:, start:stop], delta[:, start:stop]
            grad = None
            for low, high in ((start, stop), (0, start)):
                if low == high:
                    continue
                weights = jnp.exp(dot32(key_rows[low:high], columns) - shift)
                if low == start:
                    weights = jnp.where(mask, weights, 0.0)
                score = weights * (dot32(value_rows[low:high], incoming) - inner)
                score = score.astype(jnp.bfloat16)
                value_sum[low:high] += dot32(weights.astype(jnp.bfloat16), back_rows[start:stop])
                key_sum[low:high] += dot32(score, query_rows[start:stop])
                part = dot32(key_low[:, low:high], score)
                grad = part if grad is None else grad + part
            grads.append(grad * score_scale)
        out, part = head_backward(
            query_ref[at, :], query_gain_ref[...], cosine, sine, jnp.concatenate(grads, axis=1)
        )
        query_back_ref[at, :] = out.astype(jnp.bfloat16)
        query_part = query_part + part
    out, part = head_backward(key_ref[...], key_gain_ref[...], cosine, sine, key_sum[...].T)
    key_back_ref[...] = out.astype(jnp.bfloat16)
    value_back_ref[...] = value_sum[...].T.astype(jnp.bfloat16)
    query_part_ref[...] = query_part
    key_part_ref[...] = part


def group_block(rows, length):
    return pl.BlockSpec((rows, length), lambda group: (group, 0))


def shared_block(rows, length):
    return pl.BlockSpec((rows, length), lambda group: (0, 0))


def attend(query, key, value, query_gain, key_gain, cosine, sine):
    width, length = cosine.shape
    groups = key.shape[0] // width
    wide = query.shape[0] // groups
    low = jnp.bfloat16
    return pl.pallas_call(
        attend_kernel,
        grid=(groups,),
        in_specs=[
            group_block(wide, length),
            group_block(width, length),
            group_block(width, length),
            shared_block(width, 1),
            shared_block(width, 1),
            shared_block(width, length),
            shared_block(width, length),
        ],
        out_specs=[
            group_block(wide, length),
            group_block(wide, length),
            group_block(width, length),
            group_block(width, length),
            group_block(8, length),
        ],
        out_shape=[
            jax.ShapeDtypeStruct(query.shape, low),
            jax.ShapeDtypeStruct(query.shape, low),
            jax.ShapeDtypeStruct(key.shape, low),
            jax.ShapeDtypeStruct(key.shape, low),
            jax.ShapeDtypeStruct((groups * 8, length), jnp.float32),
        ],
        compiler_params=pltpu.CompilerParams(vmem_limit_bytes=VMEM_LIMIT),
        cost_estimate=SMALL_COST,
        name="attend",
    )(query, key, value, query_gain, key_gain, cosine, sine)


def attend_back(query, key, query_gain, key_gain, cosine, sine, kept, mixed_back):
    mixed, query_low, key_low, value_low, total = kept
    width, length = cosine.shape
    groups = key.shape[0] // width
    wide = query.shape[0] // groups
    low = jnp.bfloat16
    return pl.pallas_call(
        attend_back_kernel,
        grid=(groups,),
        in_specs=[
            group_block(wide, length),
            group_block(width, length),
            shared_block(width, 1),
            shared_block(width, 1),
            shared_block(width, length),
            shared_block(width, length),
            group_block(wide, length),
            group_block(width, length),
            group_block(width, length),
            group_block(wide, length),
            group_block(8, length),
            group_block(wide, length),
        ],
        out_specs=[
            group_block(wide, length),
            group_block(width, length),
            group_block(width, length),
            group_block(width, 128),
            group_block(width, 128),
        ],
        out_shape=[
            jax.ShapeDtypeStruct(query.shape, low),
            jax.ShapeDtypeStruct(key.shape, low),
            jax.ShapeDtypeStruct(key.shape, low),
            jax.ShapeDtypeStruct((groups * width, 128), jnp.float32),
            jax.ShapeDtypeStruct((groups * width, 128), jnp.float32),
        ],
        scratch_shapes=[
            pltpu.VMEM((length, width), jnp.float32),
            pltpu.VMEM((length, width), jnp.float32),
        ],
        compiler_params=pltpu.CompilerParams(vmem_limit_bytes=VMEM_LIMIT),
        cost_estimate=SMALL_COST,
        name="attend_back",
    )(query, key, query_gain, key_gain, cosine, sine, query_low, key_low, value_low, mixed, total,
      mixed_back)


def cols_dot(left, right):
    return lax.dot_general(
        left, right, (((1,), (1,)), ((), ())), preferred_element_type=jnp.float32
    )


def units_kernel(sums, *refs):
    _, normed_ref, incoming_ref, gate_ref, up_ref, down_ref, *refs = refs
    hidden_ref, gate_back_ref, up_back_ref = refs[-5:-2] if sums else refs[-3:]
    rows = normed_ref.shape[0]
    below = hidden_ref.shape[0] - rows
    if below:
        for own_ref, out_ref in zip(refs[:3], refs[3:]):
            out_ref[:below, :] = own_ref[...]
    gate_weight, up_weight, down_weight = gate_ref[...], up_ref[...], down_ref[...]
    if sums:
        mid_ref, branch_ref = refs[-2:]

        @pl.when(pl.program_id(0) == 0)
        def _():
            if sums == 2:
                mid_ref[...], branch_ref[...] = refs[0][...], refs[1][...]
            else:
                mid_ref[...] = jnp.zeros_like(mid_ref)
                branch_ref[...] = jnp.zeros_like(branch_ref)

    step = 2 * BLOCK if sums else BLOCK
    for start in range(0, rows, step):
        at = slice(start, start + step)
        normed, incoming = normed_ref[at, :], incoming_ref[at, :]
        gate_act = dot32(normed, gate_weight)
        up_act = dot32(normed, up_weight)
        hidden_back = cols_dot(incoming, down_weight)
        sigmoid = 1.0 / (1.0 + jnp.exp(-gate_act))
        silu = gate_act * sigmoid
        hidden = (silu * up_act).astype(jnp.bfloat16)
        gate_in = (hidden_back * up_act * (sigmoid + silu * (1.0 - sigmoid))).astype(jnp.bfloat16)
        up_in = (hidden_back * silu).astype(jnp.bfloat16)
        to = slice(below + start, below + start + step)
        hidden_ref[to, :] = hidden
        gate_back_ref[to, :] = gate_in
        up_back_ref[to, :] = up_in
        if sums:
            mid_ref[at, :] += cols_dot(gate_in, gate_weight) + cols_dot(up_in, up_weight)
            branch_ref[at, :] += dot32(hidden, down_weight)


def norm_kernel(halves, *refs):
    parts, (source_ref, gain_ref, middle_ref, hat_ref, low_ref) = refs[: 2 * halves], refs[2 * halves :]
    share = pl.num_programs(0) // halves

    for at in range(halves):

        @pl.when(pl.program_id(0) // share == at)
        def _(part_ref=parts[2 * at], swapped_ref=parts[2 * at + 1]):
            middle = source_ref[...].astype(jnp.float32) + (part_ref[...] + swapped_ref[...])
            scale = lax.rsqrt(jnp.mean(middle * middle, axis=-1, keepdims=True) + EPSILON)
            hat = middle * scale
            middle_ref[...] = middle
            hat_ref[...] = hat
            low_ref[...] = (hat * gain_ref[...]).astype(jnp.bfloat16)


def norm_call(parts, source, gain):
    rows, width = source.shape
    steps = rows // BLOCK
    share = steps // len(parts)

    def of_part(at):
        return pl.BlockSpec(
            (BLOCK, width), lambda step: (jnp.clip(step - at * share, 0, share - 1), 0)
        )

    block = pl.BlockSpec((BLOCK, width), lambda step: (step, 0))
    return pl.pallas_call(
        functools.partial(norm_kernel, len(parts)),
        grid=(steps,),
        in_specs=[of_part(at) for at in range(len(parts)) for _ in range(2)]
        + [block, pl.BlockSpec((1, width), lambda step: (0, 0))],
        out_specs=[block] * 3,
        out_shape=[
            jax.ShapeDtypeStruct((rows, width), jnp.float32),
            jax.ShapeDtypeStruct((rows, width), jnp.float32),
            jax.ShapeDtypeStruct((rows, width), jnp.bfloat16),
        ],
        cost_estimate=SMALL_COST,
        compiler_params=pltpu.CompilerParams(vmem_limit_bytes=VMEM_LIMIT),
        name="norm",
    )(*[array for pair in parts for array in pair], source, gain[None, :])


def norm_back_kernel(part_ref, swapped_ref, source_ref, base_ref, gain_ref, grad_ref, sum_ref, *low):
    grad = part_ref[...] + swapped_ref[...]
    source = source_ref[...].astype(jnp.float32)
    scale = lax.rsqrt(jnp.mean(source * source, axis=-1, keepdims=True) + EPSILON)
    hat = source * scale
    scaled = grad * gain_ref[...]
    inner = jnp.mean(scaled * hat, axis=-1, keepdims=True)
    out = base_ref[...].astype(jnp.float32) + scale * (scaled - hat * inner)
    grad_ref[...] = out
    for low_ref in low:
        low_ref[...] = out.astype(jnp.bfloat16)
    gains = grad * hat
    total = gains[:8]
    for at in range(8, gains.shape[0], 8):
        total = total + gains[at : at + 8]

    @pl.when(pl.program_id(0) == 0)
    def _():
        sum_ref[...] = jnp.zeros_like(sum_ref)

    sum_ref[...] += total


def norm_back_call(part, swapped, source, base, gain, rounded):
    rows, width = source.shape
    block = pl.BlockSpec((BLOCK, width), lambda step: (step, 0))
    grad, total, *low = pl.pallas_call(
        norm_back_kernel,
        grid=(rows // BLOCK,),
        in_specs=[block] * 4 + [pl.BlockSpec((1, width), lambda step: (0, 0))],
        out_specs=[block, pl.BlockSpec((8, width), lambda step: (0, 0))] + [block] * rounded,
        out_shape=[
            jax.ShapeDtypeStruct((rows, width), jnp.float32),
            jax.ShapeDtypeStruct((8, width), jnp.float32),
        ]
        + [jax.ShapeDtypeStruct((rows, width), jnp.bfloat16)] * rounded,
        cost_estimate=SMALL_COST,
        compiler_params=pltpu.CompilerParams(vmem_limit_bytes=VMEM_LIMIT),
        name="norm_back",
    )(part, swapped, source, base, gain[None, :])
    return (grad, jnp.sum(total, axis=0), *low)


def far_kernel(count, *refs):
    parts, (factor_ref, select_ref, own_ref, low_ref, left_ref) = refs[:count], refs[count:]
    rows = own_ref.shape[1]

    @pl.when(pl.program_id(0) == 0)
    def _():
        start = 0
        for part in parts:
            size = part.shape[0]
            low_ref[start : start + size, :] = (part[...] * factor_ref[...]).astype(jnp.bfloat16)
            start += size

    left_ref[:, :rows] = own_ref[...]
    left_ref[:, rows:] = cols_dot(select_ref[...], low_ref[...]).astype(jnp.bfloat16)


def far_call(parts, factor, select, own):
    width, rows = own.shape
    step = 2 * BLOCK

    def whole(shape):
        return pl.BlockSpec(shape, lambda at: (0, 0))

    by_row = pl.BlockSpec((step, rows), lambda at: (at, 0))
    return pl.pallas_call(
        functools.partial(far_kernel, len(parts)),
        grid=(width // step,),
        in_specs=[whole(part.shape) for part in parts]
        + [whole(factor.shape), pl.BlockSpec((step, width), lambda at: (at, 0)), by_row],
        out_specs=[whole((rows, width)), pl.BlockSpec((step, 2 * rows), lambda at: (at, 0))],
        out_shape=[
            jax.ShapeDtypeStruct((rows, width), jnp.bfloat16),
            jax.ShapeDtypeStruct((width, 2 * rows), jnp.bfloat16),
        ],
        cost_estimate=SMALL_COST,
        compiler_params=pltpu.CompilerParams(vmem_limit_bytes=VMEM_LIMIT),
        name="far",
    )(*parts, factor, select, own)


def units_call(
    normed, incoming, gate_weight, up_weight, down_weight, first, count, sums, start=(), own=(), skip=0
):
    rows, width = normed.shape
    wide = 3 * BLOCK
    tile = wide if sums and count % wide == 0 and first % wide == 0 else BLOCK
    low = jnp.bfloat16
    whole = pl.BlockSpec((rows, width), lambda at, base: (0, 0), pipeline_mode=pl.Buffered(1))
    by_unit = pl.BlockSpec((width, tile), lambda at, base: (0, base[0] + at))
    own_tile = pl.BlockSpec((rows, tile), lambda at, base: (0, base[1] + at))
    out_rows = 2 * rows if own else rows
    out_tile = pl.BlockSpec((out_rows, tile), lambda at, base: (0, at))
    out_shape = [jax.ShapeDtypeStruct((out_rows, count), low)] * 3
    out_specs = [out_tile] * 3
    if sums:
        out_shape = out_shape + [jax.ShapeDtypeStruct((rows, width), jnp.float32)] * 2
        out_specs = out_specs + [pl.BlockSpec((rows, width), lambda at, base: (0, 0))] * 2
    base = jnp.stack([jnp.asarray(at // tile, jnp.int32) for at in (first, skip)])
    return pl.pallas_call(
        functools.partial(units_kernel, sums),
        grid_spec=pltpu.PrefetchScalarGridSpec(
            num_scalar_prefetch=1,
            grid=(count // tile,),
            in_specs=[
                whole,
                whole,
                by_unit,
                by_unit,
                pl.BlockSpec((tile, width), lambda at, base: (base[0] + at, 0)),
            ]
            + [whole] * len(start)
            + [own_tile] * len(own),
            out_specs=out_specs,
        ),
        out_shape=out_shape,
        compiler_params=pltpu.CompilerParams(vmem_limit_bytes=VMEM_LIMIT),
        cost_estimate=SMALL_COST,
        name="units",
    )(base, normed, incoming, gate_weight, up_weight, down_weight, *start, *own)


def contract_cols(left_side, right_side):
    return lax.dot_general(
        left_side, right_side, (((1,), (1,)), ((), ())), preferred_element_type=jnp.float32
    )


def contract_rows(left_side, right_side):
    return lax.dot_general(
        left_side, right_side, (((0,), (0,)), ((), ())), preferred_element_type=jnp.float32
    )


def back_product(left_side, right_side):
    return lax.dot_general(
        left_side, right_side, (((0,), (1,)), ((), ())), preferred_element_type=jnp.float32
    )


def product(left_side, right_side):
    return jnp.dot(left_side, right_side, preferred_element_type=jnp.float32)


def swap(value, axis):
    return lax.ppermute(value, axis, SWAP)


def core_sum(value):
    return value + swap(value, "tensor")


def core_sum_halves(make, rows):
    half = rows // 2
    first, second = make(0, half), make(half, rows)
    return jnp.concatenate([core_sum(first), core_sum(second)], axis=0)


def tie(*values):
    return lax.optimization_barrier(values)


class Line:
    def __init__(self, kept, length):
        own = kept.shape[0] // length
        self.blocks = [kept[at * own : (at + 1) * own] for at in range(length)]

    def go(self, first, stop):
        length = len(self.blocks)
        return [
            lax.ppermute(
                self.blocks[away], "line", [(at, (at + away) % length) for at in range(length)]
            )
            for away in range(first, stop)
        ]


def line_sum(own, arrived):
    for part in arrived:
        own = own + part
    return own


def pair_sums(own, arrived):
    mine, other = own, None
    for away, part in enumerate(arrived, 1):
        if away % 2 == 0:
            mine = mine + part
        else:
            other = part if other is None else other + part
    return mine, other


def in_order(half, mine, other):
    return jnp.concatenate(
        [jnp.where(half == 0, mine, other), jnp.where(half == 0, other, mine)], axis=1
    )


class Plane:
    def __init__(self, pieces):
        self.pieces = pieces

    def after(self, *values):
        lefts, values = tie([piece[0] for piece in self.pieces], values)
        self.pieces = [(left, *piece[1:]) for left, piece in zip(lefts, self.pieces)]
        return values

    @staticmethod
    def rows(left, start, stop):
        quarter = left.shape[0] // 4
        return left[start * quarter : stop * quarter]

    def products(self, for_near, for_mid):
        return [
            (contract_cols if transposed else product)(
                for_near(left) if near_first else for_mid(left), right
            )
            for left, right, near_first, transposed in self.pieces
        ]

    def send(self):
        return self.products(
            lambda left: self.rows(left, 0, 2), lambda left: self.rows(left, 1, 3)
        )

    def go(self, out):
        return [
            swap(part, "near" if piece[2] else "mid") for part, piece in zip(out, self.pieces)
        ]

    def halves(self, got):
        quarter = got[0].shape[0] // 2
        return [
            (late[quarter:], late[:quarter]) if piece[2] else (late[:quarter], late[quarter:])
            for late, piece in zip(got, self.pieces)
        ]

    def follow(self, got):
        parts = self.products(lambda left: self.rows(left, 2, 3), lambda left: self.rows(left, 0, 1))
        return [part + late for part, (late, _) in zip(parts, self.halves(got))]

    def pass_on(self, out):
        return [
            swap(part, "mid" if piece[2] else "near") for part, piece in zip(out, self.pieces)
        ]

    def keep(self, got, passed):
        def own(left):
            return self.rows(left, 3, 4)

        parts = self.products(own, own)
        return jnp.concatenate(
            [
                part + early + late
                for part, (_, early), late in zip(parts, self.halves(got), passed)
            ],
            axis=1,
        )


class Owners:
    def __init__(self, width):
        self.length = lax.axis_size("line")
        self.width = width
        self.own = width // (4 * self.length)
        line, mid, near = (lax.axis_index(name) for name in ("line", "mid", "near"))
        block = lax.broadcasted_iota(jnp.int32, (4, self.length, self.own, 1), 0)
        distance = lax.broadcasted_iota(jnp.int32, block.shape, 1)
        entry = lax.broadcasted_iota(jnp.int32, block.shape, 2)
        owner_near = (near + (block < 2)) % 2
        owner_mid = (mid + (block % 3 > 0)) % 2
        owner_line = (distance + line) % self.length
        feature = ((owner_line * 2 + owner_mid) * 2 + owner_near) * self.own + entry
        column = lax.broadcasted_iota(jnp.int32, (1, width), 1)
        (self.select,) = tie((feature.reshape(width, 1) == column).astype(jnp.bfloat16))

    def plane_first(self, left):
        return contract_cols(self.select, left).astype(jnp.bfloat16)


def in_line_order(found):
    length = len(found)
    stacked = jnp.stack(found)
    total = jnp.zeros_like(found[0])
    for at in range(length):
        away = (lax.axis_index("line") - at) % length
        total = total + lax.dynamic_index_in_dim(stacked, away, 0, keepdims=False)
    return total


def local(
    inputs,
    first_gain,
    query_weight,
    key_matrix,
    value_matrix,
    query_gain,
    key_gain,
    output_weight,
    second_gain,
    gate_weight,
    up_weight,
    down_weight,
    cotangent,
):
    row_count, model_width = inputs.shape
    head_dim = query_gain.shape[0]
    units = gate_weight.shape[1]
    cosine_table, sine_table = rope_tables(row_count, head_dim)
    owners = Owners(model_width)
    length = owners.length

    core = lax.axis_index("tensor")
    half = lax.axis_index("line") % 2
    partners = [(at, at + 1 - 2 * (at % 2)) for at in range(length)]
    core_rows = row_count // 2

    def my_rows(value):
        return lax.dynamic_slice_in_dim(value, core * core_rows, core_rows, axis=0)

    def to_partner(value):
        return lax.ppermute(value, "line", partners)

    early = core_rows // 2

    def cotangent_part(start):
        part = lax.dynamic_slice_in_dim(cotangent, core * core_rows + start, early, axis=0)
        return part.astype(jnp.float32) * SHIFT

    far_first = to_partner(cotangent_part(0))
    normalized_input = rms_scale(inputs.astype(jnp.float32), first_gain).astype(jnp.bfloat16)

    def project(weight):
        return lax.dot_general(
            weight,
            normalized_input,
            (((0,), (1,)), ((), ())),
            preferred_element_type=jnp.float32,
        )

    query_proj, projected_key = project(query_weight), project(key_matrix)
    gains = (query_gain[:, None], key_gain[:, None])
    kept = attend(
        query_proj, projected_key, project(value_matrix), *gains, cosine_table, sine_table
    )
    *kept, far_first, cotangent = tie(*kept, far_first, cotangent)
    mixed = kept[0]
    far_second = to_partner(cotangent_part(early))
    attention = [
        contract_rows(mixed[:, at : at + core_rows], output_weight)
        for at in range(0, row_count, core_rows)
    ]
    middle, hat, normed_mid = norm_call(
        [(part, swap(part, "tensor")) for part in attention], inputs, second_gain
    )
    hat, normed_mid = tie(hat, normed_mid)
    hat_far = to_partner(my_rows(hat))

    weights = (gate_weight, up_weight, down_weight)

    alone = units // 3 // 256 * 256
    paired = (units - alone) // 2
    hidden_1, gate_1, up_1, *sums_1 = units_call(normed_mid, cotangent, *weights, 0, alone, 1)
    normed_left = owners.plane_first(normed_mid)
    cotangent_left = owners.plane_first(cotangent)
    plane_1 = Plane(
        [(cotangent_left, hidden_1, True, False), (normed_left, gate_1, False, False)]
    )
    sent_1 = plane_1.send()
    far = [far_first, far_second]
    sent_1, normed_mid, far, normed_left = tie(sent_1, normed_mid, far, normed_left)
    got_1 = plane_1.go(sent_1)
    far = far + [swap(part, "tensor") for part in far]
    hidden_2, gate_2, up_2, mid_part, branch_part = units_call(
        normed_mid, cotangent, *weights, alone, units - alone, 2, sums_1
    )
    got_1, mid_part, hat_far, far, up_1, normed_left = tie(
        got_1, mid_part, hat_far, far, up_1, normed_left
    )
    up_cut = alone // 256 * 128
    plane_u = Plane(
        [(normed_left, up_1[:, :up_cut], True, False), (normed_left, up_1[:, up_cut:], False, False)]
    )
    sent_u = plane_u.send()
    sent_u, got_1, hat_far, far = tie(sent_u, got_1, hat_far, far)

    got_u = plane_u.go(sent_u)
    hat_swapped = swap(hat_far, "tensor")
    follow_1 = plane_1.follow(got_1)
    far_cotangent, cotangent_both = far_call(
        far, jnp.full((1, model_width), 1.0 / SHIFT, jnp.float32), owners.select, cotangent_left
    )
    got_u, follow_1, hat_far, hat_swapped, far_cotangent, mid_part = tie(
        got_u, follow_1, hat_far, hat_swapped, far_cotangent, mid_part
    )
    passed_1 = plane_1.pass_on(follow_1)
    mid_swapped = swap(mid_part, "tensor")
    far_normed, normed_both = far_call(
        [hat_far, hat_swapped], second_gain[None, :], owners.select, normed_left
    )
    hidden_both, gate_both, up_both = units_call(
        far_normed,
        far_cotangent,
        *weights,
        alone + half * paired,
        paired,
        0,
        own=(hidden_2, gate_2, up_2),
        skip=half * paired,
    )
    passed_1, normed_both, hidden_both, gate_both, up_both, mid_swapped = tie(
        passed_1, normed_both, hidden_both, gate_both, up_both, mid_swapped
    )
    follow_u = plane_u.follow(got_u)
    follow_u, normed_both, hidden_both, gate_both, passed_1 = tie(
        follow_u, normed_both, hidden_both, gate_both, passed_1
    )
    passed_u = plane_u.pass_on(follow_u)
    plane_2 = Plane(
        [(cotangent_both, hidden_both, True, False), (normed_both, gate_both, False, False)]
    )
    sent_2 = plane_2.send()
    sent_2, passed_1, passed_u, mid_swapped = plane_u.after(
        *plane_1.after(sent_2, passed_1, passed_u, mid_swapped)
    )
    got_2 = plane_2.go(sent_2)
    line_1 = Line(
        jnp.concatenate([plane_1.keep(got_1, passed_1), plane_u.keep(got_u, passed_u)], axis=1),
        length,
    )
    moved_1 = line_1.go(1, length - 1)
    middle_grad, second_gain_grad, attention_back = norm_back_call(
        mid_part, mid_swapped, middle, cotangent, second_gain, True
    )
    mixed_back = contract_cols(output_weight, attention_back).astype(jnp.bfloat16)
    query_back, key_back, value_back, query_part, key_part = attend_back(
        query_proj, projected_key, *gains, cosine_table, sine_table, kept, mixed_back
    )
    got_2, moved_1, query_back, key_back, value_back, attention_back, up_both = tie(
        got_2, moved_1, query_back, key_back, value_back, attention_back, up_both
    )
    follow_2 = plane_2.follow(got_2)
    follow_2, attention_back, key_part, branch_part = tie(
        follow_2, attention_back, key_part, branch_part
    )
    passed_2 = plane_2.pass_on(follow_2)
    moved_1 = moved_1 + line_1.go(length - 1, length)
    head_gains = core_sum(
        jnp.concatenate(
            [
                jnp.sum(part.reshape(-1, head_dim, 128), axis=(0, 2))
                for part in (query_part, key_part)
            ]
        )
    )
    up_cut = paired * 5 // 6 // 128 * 128
    plane_3 = Plane(
        [
            (normed_both, up_both[:, :up_cut], True, False),
            (normed_both, up_both[:, up_cut:], False, False),
            (owners.plane_first(attention_back), mixed, False, True),
        ]
    )
    sent_3 = plane_3.send()
    normed_part = (
        back_product(query_back, query_weight)
        + back_product(key_back, key_matrix)
        + back_product(value_back, value_matrix)
    )
    branch_swapped = swap(branch_part, "tensor")
    passed_2, moved_1, sent_3, normed_part, head_gains, normalized_input, branch_swapped = (
        plane_2.after(
            passed_2, moved_1, sent_3, normed_part, head_gains, normalized_input, branch_swapped
        )
    )
    got_3 = plane_3.go(sent_3)
    line_2 = Line(plane_2.keep(got_2, passed_2), length)
    moved_2 = line_2.go(1, length - 1)
    input_left = owners.plane_first(normalized_input)
    plane_4 = Plane(
        [
            (input_left, jnp.concatenate([key_back, value_back], axis=0), True, True),
            (input_left, query_back, False, True),
        ]
    )
    sent_4 = plane_4.send()
    got_3, moved_2, sent_4, normed_part, branch_part, branch_swapped = tie(
        got_3, moved_2, sent_4, normed_part, branch_part, branch_swapped
    )
    follow_3 = plane_3.follow(got_3)
    follow_3, normed_part = tie(follow_3, normed_part)
    passed_3 = plane_3.pass_on(follow_3)
    moved_2 = moved_2 + line_2.go(length - 1, length)
    input_grad, first_gain_grad = norm_back_call(
        normed_part, swap(normed_part, "tensor"), inputs, middle_grad, first_gain, False
    )
    passed_3, moved_2, sent_4, input_grad, first_gain_grad, branch_part = plane_3.after(
        passed_3, moved_2, sent_4, input_grad, first_gain_grad, branch_part
    )
    got_4 = plane_4.go(sent_4)
    line_3 = Line(plane_3.keep(got_3, passed_3), length)
    moved_3 = line_3.go(1, length - 1)
    rows = jnp.stack(
        [
            first_gain_grad,
            second_gain_grad,
            jnp.pad(head_gains, (0, model_width - 2 * head_dim)),
        ]
    )
    rows = jnp.pad(rows, ((0, 5), (0, 0)))
    rows = rows + swap(rows, "near")
    result = (middle + (branch_part + branch_swapped)).astype(jnp.bfloat16)
    got_4, moved_3, rows, result = tie(got_4, moved_3, rows, result)
    follow_4 = plane_4.follow(got_4)
    follow_4, rows = tie(follow_4, rows)
    passed_4 = plane_4.pass_on(follow_4)
    moved_3 = moved_3 + line_3.go(length - 1, length)
    rows = rows + swap(rows, "mid")
    passed_4, moved_3, rows = plane_4.after(passed_4, moved_3, rows)
    line_4 = Line(plane_4.keep(got_4, passed_4), length)
    kept_rows = line_4.blocks[0].shape[0]
    line_4.blocks = [jnp.concatenate([block, rows], axis=0) for block in line_4.blocks]
    moved_4 = line_4.go(1, length)
    rows = in_line_order([rows] + [part[kept_rows:] for part in moved_4])
    attention_shard = line_sum(
        line_4.blocks[0][:kept_rows], [part[:kept_rows] for part in moved_4]
    )

    def split(total, count):
        return [total[:, at : at + count] for at in range(0, total.shape[1], count)]

    halves = [split(side, paired) for side in pair_sums(line_2.blocks[0], moved_2)]
    sides = [side[:, :paired] for side in pair_sums(line_3.blocks[0], moved_3)]
    down_2, gate_2, up_2 = (
        in_order(half, mine, other)
        for mine, other in zip(halves[0] + sides[:1], halves[1] + sides[1:])
    )
    first = line_sum(line_1.blocks[0], moved_1)
    down_1, gate_1, up_1 = split(first, alone)
    down_shard, gate_shard, up_shard = (
        jnp.concatenate(pair, axis=1)
        for pair in ((down_1, down_2), (gate_1, gate_2), (up_1, up_2))
    )
    output_shard = line_sum(
        line_3.blocks[0][:, paired:], [part[:, paired:] for part in moved_3]
    )
    key_cut = key_back.shape[0]
    pair_cut = 2 * key_cut
    index = (lax.axis_index("line") * 2 + lax.axis_index("mid")) * 2 + lax.axis_index("near")
    gains = lax.dynamic_slice(rows, (0, index * owners.own), (2, owners.own))
    return (
        result,
        input_grad,
        gains[0],
        attention_shard[:, pair_cut:],
        attention_shard[:, :key_cut],
        attention_shard[:, key_cut:pair_cut],
        rows[2, :head_dim],
        rows[2, head_dim : 2 * head_dim],
        output_shard.T,
        gains[1],
        gate_shard,
        up_shard,
        down_shard.T,
    )


def solution(mesh):
    line = mesh.shape["dp"] // 4
    shaped = Mesh(
        mesh.devices.reshape(line, 2, 2, mesh.shape["tensor"]), ("line", "mid", "near", "tensor")
    )
    dp = ("line", "mid", "near")
    placed = (
        P(dp, None),
        P(),
        P(None, "tensor"),
        P(None, "tensor"),
        P(None, "tensor"),
        P(),
        P(),
        P("tensor", None),
        P(),
        P(None, "tensor"),
        P(None, "tensor"),
        P("tensor", None),
        P(dp, None),
    )
    return jax.shard_map(
        local,
        mesh=shaped,
        in_specs=placed,
        out_specs=(
            P(dp, None),
            P(dp, None),
            P(dp),
            P(dp, "tensor"),
            P(dp, "tensor"),
            P(dp, "tensor"),
            P(),
            P(),
            P("tensor", dp),
            P(dp),
            P(dp, "tensor"),
            P(dp, "tensor"),
            P("tensor", dp),
        ),
        check_vma=False,
    )
```

```python
import functools
import math

import jax
import jax.numpy as jnp
import numpy as np
from jax import lax
from jax.experimental import pallas as pl
from jax.experimental.pallas import tpu as pltpu
from jax.sharding import Mesh, PartitionSpec as P

EPSILON = 1e-05
ROPE_BASE = 1000000.0
BLOCK = 256
NORM_ROWS = 512
SMALL_COST = pl.CostEstimate(flops=10**8, bytes_accessed=10**6, transcendentals=0)
VMEM_LIMIT = 60 * 1024 * 1024
SWAP = [(0, 1), (1, 0)]
SHIFT = 8.0


def rms_scale(values, gain):
    return values * lax.rsqrt(jnp.mean(values * values, axis=-1, keepdims=True) + EPSILON) * gain


def rope_tables(length, width):
    half_width = width // 2
    frequency = np.exp(
        np.arange(half_width, dtype=np.float32) * np.float32(-2.0 * math.log(ROPE_BASE) / width)
    )
    angles = np.arange(length, dtype=np.float32)[None, :] * frequency[:, None]
    angles = np.concatenate([angles, angles], axis=0)
    return jnp.asarray(np.cos(angles)), jnp.asarray(np.sin(angles))


def head_forward(values, gain, cosine, sine):
    scale = lax.rsqrt(jnp.mean(values * values, axis=0, keepdims=True) + EPSILON)
    normed = values * scale * gain
    half_width = values.shape[0] // 2
    turned = jnp.concatenate([-normed[half_width:], normed[:half_width]], axis=0)
    return normed * cosine + turned * sine


def head_backward(values, gain, cosine, sine, grad):
    half_width = values.shape[0] // 2
    crossed = grad * sine
    back = grad * cosine + jnp.concatenate([crossed[half_width:], -crossed[:half_width]], axis=0)
    scale = lax.rsqrt(jnp.mean(values * values, axis=0, keepdims=True) + EPSILON)
    hat = values * scale
    scaled = back * gain
    out = scale * (scaled - hat * jnp.mean(scaled * hat, axis=0, keepdims=True))
    return out, fold_lanes(back * hat)


def fold_lanes(values):
    total = values[:, :128]
    for at in range(128, values.shape[1], 128):
        total = total + values[:, at : at + 128]
    return total


def visible(size):
    key = lax.broadcasted_iota(jnp.int32, (size, size), 0)
    query = lax.broadcasted_iota(jnp.int32, (size, size), 1)
    return key <= query


def dot32(left, right):
    return jnp.dot(left, right, preferred_element_type=jnp.float32)


def attend_kernel(
    query_ref, key_ref, value_ref, query_gain_ref, key_gain_ref, cosine_ref, sine_ref,
    mixed_ref, query_low_ref, key_low_ref, value_low_ref, total_ref,
):
    width, length = key_ref.shape
    repeat = query_ref.shape[0] // width
    score_scale = width ** (-0.5)
    cosine, sine = cosine_ref[...], sine_ref[...]
    key = head_forward(key_ref[...], key_gain_ref[...], cosine, sine)
    key_low_ref[...] = key.astype(jnp.bfloat16)
    key_rows = key.T.astype(jnp.bfloat16)
    value_low = value_ref[...].astype(jnp.bfloat16)
    value_low_ref[...] = value_low
    ones = jnp.ones((16, length), jnp.bfloat16)
    value_and_one = jnp.concatenate([value_low, ones], axis=0)
    mask = visible(BLOCK)
    for head in range(repeat):
        at = slice(head * width, (head + 1) * width)
        query = head_forward(query_ref[at, :], query_gain_ref[...], cosine, sine)
        query_low = (query.astype(jnp.bfloat16).astype(jnp.float32) * score_scale).astype(
            jnp.bfloat16
        )
        query_low_ref[at, :] = query_low
        for start in range(0, length, BLOCK):
            stop = start + BLOCK
            columns = query_low[:, start:stop]
            near = jnp.exp(dot32(key_rows[start:stop], columns))
            near = jnp.where(mask, near, 0.0).astype(jnp.bfloat16)
            out = dot32(value_and_one[:, start:stop], near)
            if start:
                far = jnp.exp(dot32(key_rows[:start], columns)).astype(jnp.bfloat16)
                out = out + dot32(value_and_one[:, :start], far)
            total = out[width : width + 1]
            mixed_ref[at, start:stop] = (out[:width] / total).astype(jnp.bfloat16)
            total_ref[head : head + 1, start:stop] = jnp.log(total)


def attend_back_kernel(
    query_ref, key_ref, query_gain_ref, key_gain_ref, cosine_ref, sine_ref,
    query_low_ref, key_low_ref, value_low_ref, mixed_ref, total_ref, back_ref,
    query_back_ref, key_back_ref, value_back_ref, query_part_ref, key_part_ref,
    key_sum, value_sum,
):
    width, length = key_ref.shape
    repeat = query_ref.shape[0] // width
    score_scale = width ** (-0.5)
    cosine, sine = cosine_ref[...], sine_ref[...]

    def rows_of(value):
        return value.astype(jnp.float32).T.astype(jnp.bfloat16)

    key_low = key_low_ref[...]
    key_rows = rows_of(key_low)
    value_rows = rows_of(value_low_ref[...])
    mask = visible(BLOCK)
    key_sum[...] = jnp.zeros_like(key_sum)
    value_sum[...] = jnp.zeros_like(value_sum)
    query_part = jnp.zeros((width, 128), jnp.float32)
    for head in range(repeat):
        at = slice(head * width, (head + 1) * width)
        query_low = query_low_ref[at, :]
        query_rows = rows_of(query_low)
        back = back_ref[at, :]
        back_rows = rows_of(back)
        delta = jnp.sum(
            mixed_ref[at, :].astype(jnp.float32) * back.astype(jnp.float32), axis=0, keepdims=True
        )
        total = total_ref[head : head + 1, :]
        grads = []
        for start in range(0, length, BLOCK):
            stop = start + BLOCK
            columns, incoming = query_low[:, start:stop], back[:, start:stop]
            shift, inner = total[:, start:stop], delta[:, start:stop]
            grad = None
            for low, high in ((start, stop), (0, start)):
                if low == high:
                    continue
                weights = jnp.exp(dot32(key_rows[low:high], columns) - shift)
                if low == start:
                    weights = jnp.where(mask, weights, 0.0)
                score = weights * (dot32(value_rows[low:high], incoming) - inner)
                score = score.astype(jnp.bfloat16)
                value_sum[low:high] += dot32(weights.astype(jnp.bfloat16), back_rows[start:stop])
                key_sum[low:high] += dot32(score, query_rows[start:stop])
                part = dot32(key_low[:, low:high], score)
                grad = part if grad is None else grad + part
            grads.append(grad * score_scale)
        out, part = head_backward(
            query_ref[at, :], query_gain_ref[...], cosine, sine, jnp.concatenate(grads, axis=1)
        )
        query_back_ref[at, :] = out.astype(jnp.bfloat16)
        query_part = query_part + part
    out, part = head_backward(key_ref[...], key_gain_ref[...], cosine, sine, key_sum[...].T)
    key_back_ref[...] = out.astype(jnp.bfloat16)
    value_back_ref[...] = value_sum[...].T.astype(jnp.bfloat16)
    query_part_ref[...] = query_part
    key_part_ref[...] = part


def group_block(rows, length):
    return pl.BlockSpec((rows, length), lambda group: (group, 0))


def shared_block(rows, length):
    return pl.BlockSpec((rows, length), lambda group: (0, 0))


def attend(query, key, value, query_gain, key_gain, cosine, sine):
    width, length = cosine.shape
    groups = key.shape[0] // width
    wide = query.shape[0] // groups
    low = jnp.bfloat16
    return pl.pallas_call(
        attend_kernel,
        grid=(groups,),
        in_specs=[
            group_block(wide, length),
            group_block(width, length),
            group_block(width, length),
            shared_block(width, 1),
            shared_block(width, 1),
            shared_block(width, length),
            shared_block(width, length),
        ],
        out_specs=[
            group_block(wide, length),
            group_block(wide, length),
            group_block(width, length),
            group_block(width, length),
            group_block(8, length),
        ],
        out_shape=[
            jax.ShapeDtypeStruct(query.shape, low),
            jax.ShapeDtypeStruct(query.shape, low),
            jax.ShapeDtypeStruct(key.shape, low),
            jax.ShapeDtypeStruct(key.shape, low),
            jax.ShapeDtypeStruct((groups * 8, length), jnp.float32),
        ],
        compiler_params=pltpu.CompilerParams(vmem_limit_bytes=VMEM_LIMIT),
        cost_estimate=SMALL_COST,
        name="attend",
    )(query, key, value, query_gain, key_gain, cosine, sine)


def attend_back(query, key, query_gain, key_gain, cosine, sine, kept, mixed_back):
    mixed, query_low, key_low, value_low, total = kept
    width, length = cosine.shape
    groups = key.shape[0] // width
    wide = query.shape[0] // groups
    low = jnp.bfloat16
    return pl.pallas_call(
        attend_back_kernel,
        grid=(groups,),
        in_specs=[
            group_block(wide, length),
            group_block(width, length),
            shared_block(width, 1),
            shared_block(width, 1),
            shared_block(width, length),
            shared_block(width, length),
            group_block(wide, length),
            group_block(width, length),
            group_block(width, length),
            group_block(wide, length),
            group_block(8, length),
            group_block(wide, length),
        ],
        out_specs=[
            group_block(wide, length),
            group_block(width, length),
            group_block(width, length),
            group_block(width, 128),
            group_block(width, 128),
        ],
        out_shape=[
            jax.ShapeDtypeStruct(query.shape, low),
            jax.ShapeDtypeStruct(key.shape, low),
            jax.ShapeDtypeStruct(key.shape, low),
            jax.ShapeDtypeStruct((groups * width, 128), jnp.float32),
            jax.ShapeDtypeStruct((groups * width, 128), jnp.float32),
        ],
        scratch_shapes=[
            pltpu.VMEM((length, width), jnp.float32),
            pltpu.VMEM((length, width), jnp.float32),
        ],
        compiler_params=pltpu.CompilerParams(vmem_limit_bytes=VMEM_LIMIT),
        cost_estimate=SMALL_COST,
        name="attend_back",
    )(query, key, query_gain, key_gain, cosine, sine, query_low, key_low, value_low, mixed, total,
      mixed_back)


def cols_dot(left, right):
    return lax.dot_general(
        left, right, (((1,), (1,)), ((), ())), preferred_element_type=jnp.float32
    )


def units_kernel(sums, *refs):
    _, normed_ref, incoming_ref, gate_ref, up_ref, down_ref, *refs = refs
    hidden_ref, gate_back_ref, up_back_ref = refs[-5:-2] if sums else refs[-3:]
    rows = normed_ref.shape[0]
    below = hidden_ref.shape[0] - rows
    if below:
        for own_ref, out_ref in zip(refs[:3], refs[3:]):
            out_ref[:below, :] = own_ref[...]
    gate_weight, up_weight, down_weight = gate_ref[...], up_ref[...], down_ref[...]
    if sums:
        mid_ref, branch_ref = refs[-2:]

        @pl.when(pl.program_id(0) == 0)
        def _():
            if sums == 2:
                mid_ref[...], branch_ref[...] = refs[0][...], refs[1][...]
            else:
                mid_ref[...] = jnp.zeros_like(mid_ref)
                branch_ref[...] = jnp.zeros_like(branch_ref)

    step = 2 * BLOCK if sums else BLOCK
    for start in range(0, rows, step):
        at = slice(start, start + step)
        normed, incoming = normed_ref[at, :], incoming_ref[at, :]
        gate_act = dot32(normed, gate_weight)
        up_act = dot32(normed, up_weight)
        hidden_back = cols_dot(incoming, down_weight)
        sigmoid = 1.0 / (1.0 + jnp.exp(-gate_act))
        silu = gate_act * sigmoid
        hidden = (silu * up_act).astype(jnp.bfloat16)
        gate_in = (hidden_back * up_act * (sigmoid + silu * (1.0 - sigmoid))).astype(jnp.bfloat16)
        up_in = (hidden_back * silu).astype(jnp.bfloat16)
        to = slice(below + start, below + start + step)
        hidden_ref[to, :] = hidden
        gate_back_ref[to, :] = gate_in
        up_back_ref[to, :] = up_in
        if sums:
            mid_ref[at, :] += cols_dot(gate_in, gate_weight) + cols_dot(up_in, up_weight)
            branch_ref[at, :] += dot32(hidden, down_weight)


def norm_kernel(halves, core_ref, *refs):
    parts, (source_ref, gain_ref, middle_ref, hat_ref, low_ref) = refs[: 2 * halves], refs[2 * halves :]
    share = pl.num_programs(0) // halves

    for at in range(halves):

        @pl.when(pl.program_id(0) // share == at)
        def _(part_ref=parts[2 * at], swapped_ref=parts[2 * at + 1]):
            middle = source_ref[...].astype(jnp.float32) + (part_ref[...] + swapped_ref[...])
            scale = lax.rsqrt(jnp.mean(middle * middle, axis=-1, keepdims=True) + EPSILON)
            hat = middle * scale
            middle_ref[...] = middle
            low_ref[...] = (hat * gain_ref[...]).astype(jnp.bfloat16)

            @pl.when(core_ref[0] == at)
            def _():
                hat_ref[...] = hat


def norm_call(parts, source, gain, core):
    rows, width = source.shape
    steps = rows // NORM_ROWS
    share = steps // len(parts)

    def of_part(at):
        return pl.BlockSpec(
            (NORM_ROWS, width), lambda step, core: (jnp.clip(step - at * share, 0, share - 1), 0)
        )

    def of_core(step, core):
        return (jnp.clip(step - core[0] * share, 0, share - 1), 0)

    block = pl.BlockSpec((NORM_ROWS, width), lambda step, core: (step, 0))
    return pl.pallas_call(
        functools.partial(norm_kernel, len(parts)),
        grid_spec=pltpu.PrefetchScalarGridSpec(
            num_scalar_prefetch=1,
            grid=(steps,),
            in_specs=[of_part(at) for at in range(len(parts)) for _ in range(2)]
            + [block, pl.BlockSpec((1, width), lambda step, core: (0, 0))],
            out_specs=[block, pl.BlockSpec((NORM_ROWS, width), of_core), block],
        ),
        out_shape=[
            jax.ShapeDtypeStruct((rows, width), jnp.float32),
            jax.ShapeDtypeStruct((rows // len(parts), width), jnp.float32),
            jax.ShapeDtypeStruct((rows, width), jnp.bfloat16),
        ],
        cost_estimate=SMALL_COST,
        compiler_params=pltpu.CompilerParams(vmem_limit_bytes=VMEM_LIMIT),
        name="norm",
    )(
        jnp.asarray(core, jnp.int32).reshape(1),
        *[array for pair in parts for array in pair],
        source,
        gain[None, :],
    )


def norm_back_kernel(part_ref, swapped_ref, source_ref, base_ref, gain_ref, grad_ref, sum_ref, *low):
    grad = part_ref[...] + swapped_ref[...]
    source = source_ref[...].astype(jnp.float32)
    scale = lax.rsqrt(jnp.mean(source * source, axis=-1, keepdims=True) + EPSILON)
    hat = source * scale
    scaled = grad * gain_ref[...]
    inner = jnp.mean(scaled * hat, axis=-1, keepdims=True)
    out = base_ref[...].astype(jnp.float32) + scale * (scaled - hat * inner)
    grad_ref[...] = out
    for low_ref in low:
        low_ref[...] = out.astype(jnp.bfloat16)
    gains = grad * hat
    total = gains[:8]
    for at in range(8, gains.shape[0], 8):
        total = total + gains[at : at + 8]

    @pl.when(pl.program_id(0) == 0)
    def _():
        sum_ref[...] = jnp.zeros_like(sum_ref)

    sum_ref[...] += total


def norm_back_call(part, swapped, source, base, gain, rounded):
    rows, width = source.shape
    block = pl.BlockSpec((NORM_ROWS, width), lambda step: (step, 0))
    grad, total, *low = pl.pallas_call(
        norm_back_kernel,
        grid=(rows // NORM_ROWS,),
        in_specs=[block] * 4 + [pl.BlockSpec((1, width), lambda step: (0, 0))],
        out_specs=[block, pl.BlockSpec((8, width), lambda step: (0, 0))] + [block] * rounded,
        out_shape=[
            jax.ShapeDtypeStruct((rows, width), jnp.float32),
            jax.ShapeDtypeStruct((8, width), jnp.float32),
        ]
        + [jax.ShapeDtypeStruct((rows, width), jnp.bfloat16)] * rounded,
        cost_estimate=SMALL_COST,
        compiler_params=pltpu.CompilerParams(vmem_limit_bytes=VMEM_LIMIT),
        name="norm_back",
    )(part, swapped, source, base, gain[None, :])
    return (grad, jnp.sum(total, axis=0), *low)


def spread_kernel(query_ref, key_ref, value_ref, query_weight_ref, key_weight_ref, value_weight_ref, out_ref):
    def turned(ref):
        return ref[...].astype(jnp.float32).T.astype(jnp.bfloat16)

    out_ref[...] = (
        cols_dot(turned(query_ref), query_weight_ref[...])
        + cols_dot(turned(key_ref), key_weight_ref[...])
        + cols_dot(turned(value_ref), value_weight_ref[...])
    )


def spread_call(backs, weights):
    length = backs[0].shape[1]
    width = weights[0].shape[0]
    return pl.pallas_call(
        spread_kernel,
        grid=(length // BLOCK,),
        in_specs=[pl.BlockSpec((back.shape[0], BLOCK), lambda at: (0, at)) for back in backs]
        + [pl.BlockSpec(weight.shape, lambda at: (0, 0)) for weight in weights],
        out_specs=pl.BlockSpec((BLOCK, width), lambda at: (at, 0)),
        out_shape=jax.ShapeDtypeStruct((length, width), jnp.float32),
        cost_estimate=SMALL_COST,
        compiler_params=pltpu.CompilerParams(vmem_limit_bytes=VMEM_LIMIT),
        name="spread",
    )(*backs, *weights)


def far_kernel(count, *refs):
    parts, (factor_ref, select_ref, own_ref, low_ref, left_ref) = refs[:count], refs[count:]
    rows = own_ref.shape[1]

    @pl.when(pl.program_id(0) == 0)
    def _():
        start = 0
        for part in parts:
            size = part.shape[0]
            low_ref[start : start + size, :] = (part[...] * factor_ref[...]).astype(jnp.bfloat16)
            start += size

    left_ref[:, :rows] = own_ref[...]
    left_ref[:, rows:] = cols_dot(select_ref[...], low_ref[...]).astype(jnp.bfloat16)


def far_call(parts, factor, select, own):
    width, rows = own.shape
    step = 2 * BLOCK

    def whole(shape):
        return pl.BlockSpec(shape, lambda at: (0, 0))

    by_row = pl.BlockSpec((step, rows), lambda at: (at, 0))
    return pl.pallas_call(
        functools.partial(far_kernel, len(parts)),
        grid=(width // step,),
        in_specs=[whole(part.shape) for part in parts]
        + [whole(factor.shape), pl.BlockSpec((step, width), lambda at: (at, 0)), by_row],
        out_specs=[whole((rows, width)), pl.BlockSpec((step, 2 * rows), lambda at: (at, 0))],
        out_shape=[
            jax.ShapeDtypeStruct((rows, width), jnp.bfloat16),
            jax.ShapeDtypeStruct((width, 2 * rows), jnp.bfloat16),
        ],
        cost_estimate=SMALL_COST,
        compiler_params=pltpu.CompilerParams(vmem_limit_bytes=VMEM_LIMIT),
        name="far",
    )(*parts, factor, select, own)


def units_call(
    normed, incoming, gate_weight, up_weight, down_weight, first, count, sums, start=(), own=(), skip=0
):
    rows, width = normed.shape
    wide = 3 * BLOCK
    tile = wide if sums and count % wide == 0 and first % wide == 0 else BLOCK
    low = jnp.bfloat16
    whole = pl.BlockSpec((rows, width), lambda at, base: (0, 0), pipeline_mode=pl.Buffered(1))
    by_unit = pl.BlockSpec((width, tile), lambda at, base: (0, base[0] + at))
    own_tile = pl.BlockSpec((rows, tile), lambda at, base: (0, base[1] + at))
    out_rows = 2 * rows if own else rows
    out_tile = pl.BlockSpec((out_rows, tile), lambda at, base: (0, at))
    out_shape = [jax.ShapeDtypeStruct((out_rows, count), low)] * 3
    out_specs = [out_tile] * 3
    if sums:
        out_shape = out_shape + [jax.ShapeDtypeStruct((rows, width), jnp.float32)] * 2
        out_specs = out_specs + [pl.BlockSpec((rows, width), lambda at, base: (0, 0))] * 2
    base = jnp.stack([jnp.asarray(at // tile, jnp.int32) for at in (first, skip)])
    return pl.pallas_call(
        functools.partial(units_kernel, sums),
        grid_spec=pltpu.PrefetchScalarGridSpec(
            num_scalar_prefetch=1,
            grid=(count // tile,),
            in_specs=[
                whole,
                whole,
                by_unit,
                by_unit,
                pl.BlockSpec((tile, width), lambda at, base: (base[0] + at, 0)),
            ]
            + [whole] * len(start)
            + [own_tile] * len(own),
            out_specs=out_specs,
        ),
        out_shape=out_shape,
        compiler_params=pltpu.CompilerParams(vmem_limit_bytes=VMEM_LIMIT),
        cost_estimate=SMALL_COST,
        name="units",
    )(base, normed, incoming, gate_weight, up_weight, down_weight, *start, *own)


def contract_cols(left_side, right_side):
    return lax.dot_general(
        left_side, right_side, (((1,), (1,)), ((), ())), preferred_element_type=jnp.float32
    )


def contract_rows(left_side, right_side):
    return lax.dot_general(
        left_side, right_side, (((0,), (0,)), ((), ())), preferred_element_type=jnp.float32
    )


def product(left_side, right_side):
    return jnp.dot(left_side, right_side, preferred_element_type=jnp.float32)


def swap(value, axis):
    return lax.ppermute(value, axis, SWAP)


def core_sum(value):
    return value + swap(value, "tensor")


def core_sum_halves(make, rows):
    half = rows // 2
    first, second = make(0, half), make(half, rows)
    return jnp.concatenate([core_sum(first), core_sum(second)], axis=0)


def tie(*values):
    return lax.optimization_barrier(values)


class Line:
    def __init__(self, kept, length):
        own = kept.shape[0] // length
        self.blocks = [kept[at * own : (at + 1) * own] for at in range(length)]

    def go(self, aways):
        length = len(self.blocks)
        return {
            away: lax.ppermute(
                self.blocks[away], "line", [(at, (at + away) % length) for at in range(length)]
            )
            for away in aways
        }


def by_distance(*moved):
    together = {away: part for one in moved for away, part in one.items()}
    return [together[away] for away in sorted(together)]


def line_sum(own, arrived):
    for part in arrived:
        own = own + part
    return own


def pair_sums(own, arrived):
    mine, other = own, None
    for away, part in enumerate(arrived, 1):
        if away % 2 == 0:
            mine = mine + part
        else:
            other = part if other is None else other + part
    return mine, other


def in_order(half, mine, other):
    return jnp.concatenate(
        [jnp.where(half == 0, mine, other), jnp.where(half == 0, other, mine)], axis=1
    )


class Plane:
    def __init__(self, pieces):
        self.pieces = pieces

    def after(self, *values):
        lefts, values = tie([piece[0] for piece in self.pieces], values)
        self.pieces = [(left, *piece[1:]) for left, piece in zip(lefts, self.pieces)]
        return values

    @staticmethod
    def rows(left, start, stop):
        quarter = left.shape[0] // 4
        return left[start * quarter : stop * quarter]

    def products(self, for_near, for_mid):
        return [
            (contract_cols if transposed else product)(
                for_near(left) if near_first else for_mid(left), right
            )
            for left, right, near_first, transposed in self.pieces
        ]

    def send(self):
        return self.products(
            lambda left: self.rows(left, 0, 2), lambda left: self.rows(left, 1, 3)
        )

    def go(self, out):
        return [
            swap(part, "near" if piece[2] else "mid") for part, piece in zip(out, self.pieces)
        ]

    def halves(self, got):
        quarter = got[0].shape[0] // 2
        return [
            (late[quarter:], late[:quarter]) if piece[2] else (late[:quarter], late[quarter:])
            for late, piece in zip(got, self.pieces)
        ]

    def follow(self, got):
        parts = self.products(lambda left: self.rows(left, 2, 3), lambda left: self.rows(left, 0, 1))
        return [part + late for part, (late, _) in zip(parts, self.halves(got))]

    def pass_on(self, out):
        return [
            swap(part, "mid" if piece[2] else "near") for part, piece in zip(out, self.pieces)
        ]

    def keep(self, got, passed):
        def own(left):
            return self.rows(left, 3, 4)

        parts = self.products(own, own)
        return jnp.concatenate(
            [
                part + early + late
                for part, (_, early), late in zip(parts, self.halves(got), passed)
            ],
            axis=1,
        )


class Owners:
    def __init__(self, width):
        self.length = lax.axis_size("line")
        self.width = width
        self.own = width // (4 * self.length)
        line, mid, near = (lax.axis_index(name) for name in ("line", "mid", "near"))
        block = lax.broadcasted_iota(jnp.int32, (4, self.length, self.own, 1), 0)
        distance = lax.broadcasted_iota(jnp.int32, block.shape, 1)
        entry = lax.broadcasted_iota(jnp.int32, block.shape, 2)
        owner_near = (near + (block < 2)) % 2
        owner_mid = (mid + (block % 3 > 0)) % 2
        owner_line = (distance + line) % self.length
        feature = ((owner_line * 2 + owner_mid) * 2 + owner_near) * self.own + entry
        column = lax.broadcasted_iota(jnp.int32, (1, width), 1)
        (self.select,) = tie((feature.reshape(width, 1) == column).astype(jnp.bfloat16))

    def plane_first(self, left):
        return contract_cols(self.select, left).astype(jnp.bfloat16)


def in_line_order(found):
    length = len(found)
    stacked = jnp.stack(found)
    total = jnp.zeros_like(found[0])
    for at in range(length):
        away = (lax.axis_index("line") - at) % length
        total = total + lax.dynamic_index_in_dim(stacked, away, 0, keepdims=False)
    return total


def local(
    inputs,
    first_gain,
    query_weight,
    key_matrix,
    value_matrix,
    query_gain,
    key_gain,
    output_weight,
    second_gain,
    gate_weight,
    up_weight,
    down_weight,
    cotangent,
):
    row_count, model_width = inputs.shape
    head_dim = query_gain.shape[0]
    units = gate_weight.shape[1]
    cosine_table, sine_table = rope_tables(row_count, head_dim)
    owners = Owners(model_width)
    length = owners.length
    far_away = [length // 2]
    other_away = [away for away in range(1, length) if away != length // 2]

    core = lax.axis_index("tensor")
    half = lax.axis_index("line") % 2
    partners = [(at, at + 1 - 2 * (at % 2)) for at in range(length)]
    core_rows = row_count // 2

    def to_partner(value):
        return lax.ppermute(value, "line", partners)

    early = core_rows // 2

    def cotangent_part(start):
        part = lax.dynamic_slice_in_dim(cotangent, core * core_rows + start, early, axis=0)
        return part.astype(jnp.float32) * SHIFT

    far_first = to_partner(cotangent_part(0))
    normalized_input = rms_scale(inputs.astype(jnp.float32), first_gain).astype(jnp.bfloat16)

    def project(weight):
        return lax.dot_general(
            weight,
            normalized_input,
            (((0,), (1,)), ((), ())),
            preferred_element_type=jnp.float32,
        )

    query_proj, projected_key = project(query_weight), project(key_matrix)
    gains = (query_gain[:, None], key_gain[:, None])
    kept = attend(
        query_proj, projected_key, project(value_matrix), *gains, cosine_table, sine_table
    )
    *kept, far_first, cotangent = tie(*kept, far_first, cotangent)
    mixed = kept[0]
    far_second = to_partner(cotangent_part(early))
    attention = [
        contract_rows(mixed[:, at : at + core_rows], output_weight)
        for at in range(0, row_count, core_rows)
    ]
    middle, hat, normed_mid = norm_call(
        [(part, swap(part, "tensor")) for part in attention], inputs, second_gain, core
    )
    hat, normed_mid = tie(hat, normed_mid)
    hat_far = to_partner(hat)

    weights = (gate_weight, up_weight, down_weight)

    alone = units // 3 // 256 * 256
    paired = (units - alone) // 2
    hidden_1, gate_1, up_1, *sums_1 = units_call(normed_mid, cotangent, *weights, 0, alone, 1)
    normed_left = owners.plane_first(normed_mid)
    cotangent_left = owners.plane_first(cotangent)
    plane_1 = Plane(
        [(cotangent_left, hidden_1, True, False), (normed_left, gate_1, False, False)]
    )
    sent_1 = plane_1.send()
    far = [far_first, far_second]
    sent_1, normed_mid, far, normed_left = tie(sent_1, normed_mid, far, normed_left)
    got_1 = plane_1.go(sent_1)
    far = far + [swap(part, "tensor") for part in far]
    hidden_2, gate_2, up_2, mid_part, branch_part = units_call(
        normed_mid, cotangent, *weights, alone, units - alone, 2, sums_1
    )
    got_1, mid_part, hat_far, far, up_1, normed_left = tie(
        got_1, mid_part, hat_far, far, up_1, normed_left
    )
    up_cut = alone // 256 * 128
    plane_u = Plane(
        [(normed_left, up_1[:, :up_cut], True, False), (normed_left, up_1[:, up_cut:], False, False)]
    )
    sent_u = plane_u.send()
    sent_u, got_1, hat_far, far = tie(sent_u, got_1, hat_far, far)

    got_u = plane_u.go(sent_u)
    hat_swapped = swap(hat_far, "tensor")
    follow_1 = plane_1.follow(got_1)
    far_cotangent, cotangent_both = far_call(
        far, jnp.full((1, model_width), 1.0 / SHIFT, jnp.float32), owners.select, cotangent_left
    )
    far_normed, normed_both = far_call(
        [hat_far, hat_swapped], second_gain[None, :], owners.select, normed_left
    )
    got_u, follow_1, far_normed, normed_both, far_cotangent, mid_part = tie(
        got_u, follow_1, far_normed, normed_both, far_cotangent, mid_part
    )
    passed_1 = plane_1.pass_on(follow_1)
    mid_swapped = swap(mid_part, "tensor")
    hidden_both, gate_both, up_both = units_call(
        far_normed,
        far_cotangent,
        *weights,
        alone + half * paired,
        paired,
        0,
        own=(hidden_2, gate_2, up_2),
        skip=half * paired,
    )
    passed_1, normed_both, hidden_both, gate_both, up_both, mid_swapped = tie(
        passed_1, normed_both, hidden_both, gate_both, up_both, mid_swapped
    )
    follow_u = plane_u.follow(got_u)
    follow_u, normed_both, hidden_both, gate_both, passed_1 = tie(
        follow_u, normed_both, hidden_both, gate_both, passed_1
    )
    passed_u = plane_u.pass_on(follow_u)
    plane_2 = Plane(
        [(cotangent_both, hidden_both, True, False), (normed_both, gate_both, False, False)]
    )
    sent_2 = plane_2.send()
    sent_2, passed_1, passed_u, mid_swapped, up_both, normalized_input = plane_u.after(
        *plane_1.after(sent_2, passed_1, passed_u, mid_swapped, up_both, normalized_input)
    )
    got_2 = plane_2.go(sent_2)
    line_1 = Line(
        jnp.concatenate([plane_1.keep(got_1, passed_1), plane_u.keep(got_u, passed_u)], axis=1),
        length,
    )
    moved_1 = line_1.go(other_away)
    middle_grad, second_gain_grad, attention_back = norm_back_call(
        mid_part, mid_swapped, middle, cotangent, second_gain, True
    )
    mixed_back = contract_cols(output_weight, attention_back).astype(jnp.bfloat16)
    up_cut = paired * 5 // 6 // 128 * 128
    plane_3 = Plane(
        [
            (normed_both, up_both[:, :up_cut], True, False),
            (normed_both, up_both[:, up_cut:], False, False),
            (owners.plane_first(attention_back), mixed, False, True),
        ]
    )
    sent_3 = plane_3.send()
    branch_swapped = swap(branch_part, "tensor")
    got_2, moved_1, mixed_back, sent_3, normalized_input, branch_swapped = tie(
        got_2, moved_1, mixed_back, sent_3, normalized_input, branch_swapped
    )
    follow_2 = plane_2.follow(got_2)
    follow_2, mixed_back, branch_part = tie(follow_2, mixed_back, branch_part)
    passed_2 = plane_2.pass_on(follow_2)
    later_1 = line_1.go(far_away)
    query_back, key_back, value_back, query_part, key_part = attend_back(
        query_proj, projected_key, *gains, cosine_table, sine_table, kept, mixed_back
    )
    normed_part = spread_call(
        (query_back, key_back, value_back), (query_weight, key_matrix, value_matrix)
    )
    passed_2, moved_1, later_1, sent_3, query_back, key_back, value_back, normalized_input = (
        plane_2.after(
            passed_2, moved_1, later_1, sent_3, query_back, key_back, value_back, normalized_input
        )
    )
    got_3 = plane_3.go(sent_3)
    line_2 = Line(plane_2.keep(got_2, passed_2), length)
    moved_2 = line_2.go(other_away)
    got_3, moved_2, normed_part, branch_part, branch_swapped = tie(
        got_3, moved_2, normed_part, branch_part, branch_swapped
    )
    follow_3 = plane_3.follow(got_3)
    head_gains = core_sum(
        jnp.concatenate(
            [
                jnp.sum(part.reshape(-1, head_dim, 128), axis=(0, 2))
                for part in (query_part, key_part)
            ]
        )
    )
    follow_3, normed_part, head_gains, normalized_input = tie(
        follow_3, normed_part, head_gains, normalized_input
    )
    passed_3 = plane_3.pass_on(follow_3)
    later_2 = line_2.go(far_away)
    input_left = owners.plane_first(normalized_input)
    plane_4 = Plane(
        [
            (input_left, jnp.concatenate([key_back, value_back], axis=0), True, True),
            (input_left, query_back, False, True),
        ]
    )
    sent_4 = plane_4.send()
    input_grad, first_gain_grad = norm_back_call(
        normed_part, swap(normed_part, "tensor"), inputs, middle_grad, first_gain, False
    )
    rows = jnp.stack(
        [
            first_gain_grad,
            second_gain_grad,
            jnp.pad(head_gains, (0, model_width - 2 * head_dim)),
        ]
    )
    rows = jnp.pad(rows, ((0, 5), (0, 0)))
    passed_3, moved_1, later_1, moved_2, later_2, sent_4, input_grad, rows, branch_part = (
        plane_3.after(
            passed_3, moved_1, later_1, moved_2, later_2, sent_4, input_grad, rows, branch_part
        )
    )
    got_4 = plane_4.go(sent_4)
    line_3 = Line(plane_3.keep(got_3, passed_3), length)
    moved_3 = line_3.go(other_away)
    rows = rows + swap(rows, "near")
    got_4, moved_3, rows, branch_part = tie(got_4, moved_3, rows, branch_part)
    follow_4 = plane_4.follow(got_4)
    follow_4, rows = tie(follow_4, rows)
    passed_4 = plane_4.pass_on(follow_4)
    result = (middle + (branch_part + branch_swapped)).astype(jnp.bfloat16)
    later_3 = line_3.go(far_away)
    rows = rows + swap(rows, "mid")
    passed_4, moved_1, later_1, moved_2, later_2, moved_3, later_3, rows, result = plane_4.after(
        passed_4, moved_1, later_1, moved_2, later_2, moved_3, later_3, rows, result
    )
    line_4 = Line(plane_4.keep(got_4, passed_4), length)
    kept_rows = line_4.blocks[0].shape[0]
    line_4.blocks = [jnp.concatenate([block, rows], axis=0) for block in line_4.blocks]
    moved_4 = by_distance(line_4.go(range(1, length)))
    rows = in_line_order([rows] + [part[kept_rows:] for part in moved_4])
    attention_shard = line_sum(
        line_4.blocks[0][:kept_rows], [part[:kept_rows] for part in moved_4]
    )

    def split(total, count):
        return [total[:, at : at + count] for at in range(0, total.shape[1], count)]

    halves = [split(side, paired) for side in pair_sums(line_2.blocks[0], by_distance(moved_2, later_2))]
    moved_3 = by_distance(moved_3, later_3)
    sides = [side[:, :paired] for side in pair_sums(line_3.blocks[0], moved_3)]
    down_2, gate_2, up_2 = (
        in_order(half, mine, other)
        for mine, other in zip(halves[0] + sides[:1], halves[1] + sides[1:])
    )
    first = line_sum(line_1.blocks[0], by_distance(moved_1, later_1))
    down_1, gate_1, up_1 = split(first, alone)
    down_shard, gate_shard, up_shard = (
        jnp.concatenate(pair, axis=1)
        for pair in ((down_1, down_2), (gate_1, gate_2), (up_1, up_2))
    )
    output_shard = line_sum(
        line_3.blocks[0][:, paired:], [part[:, paired:] for part in moved_3]
    )
    key_cut = key_back.shape[0]
    pair_cut = 2 * key_cut
    index = (lax.axis_index("line") * 2 + lax.axis_index("mid")) * 2 + lax.axis_index("near")
    gains = lax.dynamic_slice(rows, (0, index * owners.own), (2, owners.own))
    return (
        result,
        input_grad,
        gains[0],
        attention_shard[:, pair_cut:],
        attention_shard[:, :key_cut],
        attention_shard[:, key_cut:pair_cut],
        rows[2, :head_dim],
        rows[2, head_dim : 2 * head_dim],
        output_shard.T,
        gains[1],
        gate_shard,
        up_shard,
        down_shard.T,
    )


def solution(mesh):
    line = mesh.shape["dp"] // 4
    shaped = Mesh(
        mesh.devices.reshape(line, 2, 2, mesh.shape["tensor"]), ("line", "mid", "near", "tensor")
    )
    dp = ("line", "mid", "near")
    placed = (
        P(dp, None),
        P(),
        P(None, "tensor"),
        P(None, "tensor"),
        P(None, "tensor"),
        P(),
        P(),
        P("tensor", None),
        P(),
        P(None, "tensor"),
        P(None, "tensor"),
        P("tensor", None),
        P(dp, None),
    )
    return jax.shard_map(
        local,
        mesh=shaped,
        in_specs=placed,
        out_specs=(
            P(dp, None),
            P(dp, None),
            P(dp),
            P(dp, "tensor"),
            P(dp, "tensor"),
            P(dp, "tensor"),
            P(),
            P(),
            P("tensor", dp),
            P(dp),
            P(dp, "tensor"),
            P(dp, "tensor"),
            P("tensor", dp),
        ),
        check_vma=False,
    )
```

```python
import functools
import math

import jax
import jax.numpy as jnp
import numpy as np
from jax import lax
from jax.experimental import pallas as pl
from jax.experimental.pallas import tpu as pltpu
from jax.sharding import Mesh, PartitionSpec as P

EPSILON = 1e-05
ROPE_BASE = 1000000.0
BLOCK = 256
NORM_ROWS = 512
SMALL_COST = pl.CostEstimate(flops=10**8, bytes_accessed=10**6, transcendentals=0)
VMEM_LIMIT = 60 * 1024 * 1024
SWAP = [(0, 1), (1, 0)]
SHIFT = 8.0


def rms_scale(values, gain):
    return values * lax.rsqrt(jnp.mean(values * values, axis=-1, keepdims=True) + EPSILON) * gain


def rope_tables(length, width):
    half_width = width // 2
    frequency = np.exp(
        np.arange(half_width, dtype=np.float32) * np.float32(-2.0 * math.log(ROPE_BASE) / width)
    )
    angles = np.arange(length, dtype=np.float32)[None, :] * frequency[:, None]
    angles = np.concatenate([angles, angles], axis=0)
    return jnp.asarray(np.cos(angles)), jnp.asarray(np.sin(angles))


def head_forward(values, gain, cosine, sine):
    scale = lax.rsqrt(jnp.mean(values * values, axis=0, keepdims=True) + EPSILON)
    normed = values * scale * gain
    half_width = values.shape[0] // 2
    turned = jnp.concatenate([-normed[half_width:], normed[:half_width]], axis=0)
    return normed * cosine + turned * sine


def head_backward(values, gain, cosine, sine, grad):
    half_width = values.shape[0] // 2
    crossed = grad * sine
    back = grad * cosine + jnp.concatenate([crossed[half_width:], -crossed[:half_width]], axis=0)
    scale = lax.rsqrt(jnp.mean(values * values, axis=0, keepdims=True) + EPSILON)
    hat = values * scale
    scaled = back * gain
    out = scale * (scaled - hat * jnp.mean(scaled * hat, axis=0, keepdims=True))
    return out, fold_lanes(back * hat)


def fold_lanes(values):
    total = values[:, :128]
    for at in range(128, values.shape[1], 128):
        total = total + values[:, at : at + 128]
    return total


def visible(size):
    key = lax.broadcasted_iota(jnp.int32, (size, size), 0)
    query = lax.broadcasted_iota(jnp.int32, (size, size), 1)
    return key <= query


def dot32(left, right):
    return jnp.dot(left, right, preferred_element_type=jnp.float32)


def attend_kernel(
    query_ref, key_ref, value_ref, query_gain_ref, key_gain_ref, cosine_ref, sine_ref,
    mixed_ref, query_low_ref, key_low_ref, value_low_ref, total_ref,
):
    width, length = key_ref.shape
    repeat = query_ref.shape[0] // width
    score_scale = width ** (-0.5)
    cosine, sine = cosine_ref[...], sine_ref[...]
    key = head_forward(key_ref[...], key_gain_ref[...], cosine, sine)
    key_low_ref[...] = key.astype(jnp.bfloat16)
    key_rows = key.T.astype(jnp.bfloat16)
    value_low = value_ref[...].astype(jnp.bfloat16)
    value_low_ref[...] = value_low
    ones = jnp.ones((16, length), jnp.bfloat16)
    value_and_one = jnp.concatenate([value_low, ones], axis=0)
    mask = visible(BLOCK)
    for head in range(repeat):
        at = slice(head * width, (head + 1) * width)
        query = head_forward(query_ref[at, :], query_gain_ref[...], cosine, sine)
        query_low = (query.astype(jnp.bfloat16).astype(jnp.float32) * score_scale).astype(
            jnp.bfloat16
        )
        query_low_ref[at, :] = query_low
        for start in range(0, length, BLOCK):
            stop = start + BLOCK
            columns = query_low[:, start:stop]
            near = jnp.exp(dot32(key_rows[start:stop], columns))
            near = jnp.where(mask, near, 0.0).astype(jnp.bfloat16)
            out = dot32(value_and_one[:, start:stop], near)
            if start:
                far = jnp.exp(dot32(key_rows[:start], columns)).astype(jnp.bfloat16)
                out = out + dot32(value_and_one[:, :start], far)
            total = out[width : width + 1]
            mixed_ref[at, start:stop] = (out[:width] / total).astype(jnp.bfloat16)
            total_ref[head : head + 1, start:stop] = jnp.log(total)


def attend_back_kernel(
    query_ref, key_ref, query_gain_ref, key_gain_ref, cosine_ref, sine_ref,
    query_low_ref, key_low_ref, value_low_ref, mixed_ref, total_ref, back_ref,
    query_back_ref, key_back_ref, value_back_ref, query_part_ref, key_part_ref,
    key_sum, value_sum,
):
    width, length = key_ref.shape
    repeat = query_ref.shape[0] // width
    score_scale = width ** (-0.5)
    cosine, sine = cosine_ref[...], sine_ref[...]

    def rows_of(value):
        return value.astype(jnp.float32).T.astype(jnp.bfloat16)

    key_low = key_low_ref[...]
    key_rows = rows_of(key_low)
    value_rows = rows_of(value_low_ref[...])
    mask = visible(BLOCK)
    key_sum[...] = jnp.zeros_like(key_sum)
    value_sum[...] = jnp.zeros_like(value_sum)
    query_part = jnp.zeros((width, 128), jnp.float32)
    for head in range(repeat):
        at = slice(head * width, (head + 1) * width)
        query_low = query_low_ref[at, :]
        query_rows = rows_of(query_low)
        back = back_ref[at, :]
        back_rows = rows_of(back)
        delta = jnp.sum(
            mixed_ref[at, :].astype(jnp.float32) * back.astype(jnp.float32), axis=0, keepdims=True
        )
        total = total_ref[head : head + 1, :]
        grads = []
        for start in range(0, length, BLOCK):
            stop = start + BLOCK
            columns, incoming = query_low[:, start:stop], back[:, start:stop]
            shift, inner = total[:, start:stop], delta[:, start:stop]
            grad = None
            for low, high in ((start, stop), (0, start)):
                if low == high:
                    continue
                weights = jnp.exp(dot32(key_rows[low:high], columns) - shift)
                if low == start:
                    weights = jnp.where(mask, weights, 0.0)
                score = weights * (dot32(value_rows[low:high], incoming) - inner)
                score = score.astype(jnp.bfloat16)
                value_sum[low:high] += dot32(weights.astype(jnp.bfloat16), back_rows[start:stop])
                key_sum[low:high] += dot32(score, query_rows[start:stop])
                part = dot32(key_low[:, low:high], score)
                grad = part if grad is None else grad + part
            grads.append(grad * score_scale)
        out, part = head_backward(
            query_ref[at, :], query_gain_ref[...], cosine, sine, jnp.concatenate(grads, axis=1)
        )
        query_back_ref[at, :] = out.astype(jnp.bfloat16)
        query_part = query_part + part
    out, part = head_backward(key_ref[...], key_gain_ref[...], cosine, sine, key_sum[...].T)
    key_back_ref[...] = out.astype(jnp.bfloat16)
    value_back_ref[...] = value_sum[...].T.astype(jnp.bfloat16)
    query_part_ref[...] = query_part
    key_part_ref[...] = part


def group_block(rows, length):
    return pl.BlockSpec((rows, length), lambda group: (group, 0))


def shared_block(rows, length):
    return pl.BlockSpec((rows, length), lambda group: (0, 0))


def attend(query, key, value, query_gain, key_gain, cosine, sine):
    width, length = cosine.shape
    groups = key.shape[0] // width
    wide = query.shape[0] // groups
    low = jnp.bfloat16
    return pl.pallas_call(
        attend_kernel,
        grid=(groups,),
        in_specs=[
            group_block(wide, length),
            group_block(width, length),
            group_block(width, length),
            shared_block(width, 1),
            shared_block(width, 1),
            shared_block(width, length),
            shared_block(width, length),
        ],
        out_specs=[
            group_block(wide, length),
            group_block(wide, length),
            group_block(width, length),
            group_block(width, length),
            group_block(8, length),
        ],
        out_shape=[
            jax.ShapeDtypeStruct(query.shape, low),
            jax.ShapeDtypeStruct(query.shape, low),
            jax.ShapeDtypeStruct(key.shape, low),
            jax.ShapeDtypeStruct(key.shape, low),
            jax.ShapeDtypeStruct((groups * 8, length), jnp.float32),
        ],
        compiler_params=pltpu.CompilerParams(vmem_limit_bytes=VMEM_LIMIT),
        cost_estimate=SMALL_COST,
        name="attend",
    )(query, key, value, query_gain, key_gain, cosine, sine)


def attend_back(query, key, query_gain, key_gain, cosine, sine, kept, mixed_back):
    mixed, query_low, key_low, value_low, total = kept
    width, length = cosine.shape
    groups = key.shape[0] // width
    wide = query.shape[0] // groups
    low = jnp.bfloat16
    return pl.pallas_call(
        attend_back_kernel,
        grid=(groups,),
        in_specs=[
            group_block(wide, length),
            group_block(width, length),
            shared_block(width, 1),
            shared_block(width, 1),
            shared_block(width, length),
            shared_block(width, length),
            group_block(wide, length),
            group_block(width, length),
            group_block(width, length),
            group_block(wide, length),
            group_block(8, length),
            group_block(wide, length),
        ],
        out_specs=[
            group_block(wide, length),
            group_block(width, length),
            group_block(width, length),
            group_block(width, 128),
            group_block(width, 128),
        ],
        out_shape=[
            jax.ShapeDtypeStruct(query.shape, low),
            jax.ShapeDtypeStruct(key.shape, low),
            jax.ShapeDtypeStruct(key.shape, low),
            jax.ShapeDtypeStruct((groups * width, 128), jnp.float32),
            jax.ShapeDtypeStruct((groups * width, 128), jnp.float32),
        ],
        scratch_shapes=[
            pltpu.VMEM((length, width), jnp.float32),
            pltpu.VMEM((length, width), jnp.float32),
        ],
        compiler_params=pltpu.CompilerParams(vmem_limit_bytes=VMEM_LIMIT),
        cost_estimate=SMALL_COST,
        name="attend_back",
    )(query, key, query_gain, key_gain, cosine, sine, query_low, key_low, value_low, mixed, total,
      mixed_back)


def cols_dot(left, right):
    return lax.dot_general(
        left, right, (((1,), (1,)), ((), ())), preferred_element_type=jnp.float32
    )


def units_kernel(sums, *refs):
    _, normed_ref, incoming_ref, gate_ref, up_ref, down_ref, *refs = refs
    hidden_ref, gate_back_ref, up_back_ref = refs[-5:-2] if sums else refs[-3:]
    rows = normed_ref.shape[0]
    below = hidden_ref.shape[0] - rows
    if below:
        for own_ref, out_ref in zip(refs[:3], refs[3:]):
            out_ref[:below, :] = own_ref[...]
    gate_weight, up_weight, down_weight = gate_ref[...], up_ref[...], down_ref[...]
    if sums:
        mid_ref, branch_ref = refs[-2:]

        @pl.when(pl.program_id(0) == 0)
        def _():
            if sums == 2:
                mid_ref[...], branch_ref[...] = refs[0][...], refs[1][...]
            else:
                mid_ref[...] = jnp.zeros_like(mid_ref)
                branch_ref[...] = jnp.zeros_like(branch_ref)

    step = 2 * BLOCK if sums else BLOCK
    for start in range(0, rows, step):
        at = slice(start, start + step)
        normed, incoming = normed_ref[at, :], incoming_ref[at, :]
        gate_act = dot32(normed, gate_weight)
        up_act = dot32(normed, up_weight)
        hidden_back = cols_dot(incoming, down_weight)
        sigmoid = 1.0 / (1.0 + jnp.exp(-gate_act))
        silu = gate_act * sigmoid
        hidden = (silu * up_act).astype(jnp.bfloat16)
        gate_in = (hidden_back * up_act * (sigmoid + silu * (1.0 - sigmoid))).astype(jnp.bfloat16)
        up_in = (hidden_back * silu).astype(jnp.bfloat16)
        to = slice(below + start, below + start + step)
        hidden_ref[to, :] = hidden
        gate_back_ref[to, :] = gate_in
        up_back_ref[to, :] = up_in
        if sums:
            mid_ref[at, :] += cols_dot(gate_in, gate_weight) + cols_dot(up_in, up_weight)
            branch_ref[at, :] += dot32(hidden, down_weight)


def norm_kernel(halves, core_ref, *refs):
    parts, (source_ref, gain_ref, middle_ref, hat_ref, low_ref) = refs[: 2 * halves], refs[2 * halves :]
    share = pl.num_programs(0) // halves

    for at in range(halves):

        @pl.when(pl.program_id(0) // share == at)
        def _(part_ref=parts[2 * at], swapped_ref=parts[2 * at + 1]):
            middle = source_ref[...].astype(jnp.float32) + (part_ref[...] + swapped_ref[...])
            scale = lax.rsqrt(jnp.mean(middle * middle, axis=-1, keepdims=True) + EPSILON)
            hat = middle * scale
            middle_ref[...] = middle
            low_ref[...] = (hat * gain_ref[...]).astype(jnp.bfloat16)

            @pl.when(core_ref[0] == at)
            def _():
                hat_ref[...] = hat


def norm_call(parts, source, gain, core):
    rows, width = source.shape
    steps = rows // NORM_ROWS
    share = steps // len(parts)

    def of_part(at):
        return pl.BlockSpec(
            (NORM_ROWS, width), lambda step, core: (jnp.clip(step - at * share, 0, share - 1), 0)
        )

    def of_core(step, core):
        return (jnp.clip(step - core[0] * share, 0, share - 1), 0)

    block = pl.BlockSpec((NORM_ROWS, width), lambda step, core: (step, 0))
    return pl.pallas_call(
        functools.partial(norm_kernel, len(parts)),
        grid_spec=pltpu.PrefetchScalarGridSpec(
            num_scalar_prefetch=1,
            grid=(steps,),
            in_specs=[of_part(at) for at in range(len(parts)) for _ in range(2)]
            + [block, pl.BlockSpec((1, width), lambda step, core: (0, 0))],
            out_specs=[block, pl.BlockSpec((NORM_ROWS, width), of_core), block],
        ),
        out_shape=[
            jax.ShapeDtypeStruct((rows, width), jnp.float32),
            jax.ShapeDtypeStruct((rows // len(parts), width), jnp.float32),
            jax.ShapeDtypeStruct((rows, width), jnp.bfloat16),
        ],
        cost_estimate=SMALL_COST,
        compiler_params=pltpu.CompilerParams(vmem_limit_bytes=VMEM_LIMIT),
        name="norm",
    )(
        jnp.asarray(core, jnp.int32).reshape(1),
        *[array for pair in parts for array in pair],
        source,
        gain[None, :],
    )


def norm_back_kernel(part_ref, swapped_ref, source_ref, base_ref, gain_ref, grad_ref, sum_ref, *low):
    grad = part_ref[...] + swapped_ref[...]
    source = source_ref[...].astype(jnp.float32)
    scale = lax.rsqrt(jnp.mean(source * source, axis=-1, keepdims=True) + EPSILON)
    hat = source * scale
    scaled = grad * gain_ref[...]
    inner = jnp.mean(scaled * hat, axis=-1, keepdims=True)
    out = base_ref[...].astype(jnp.float32) + scale * (scaled - hat * inner)
    grad_ref[...] = out
    for low_ref in low:
        low_ref[...] = out.astype(jnp.bfloat16)
    gains = grad * hat
    total = gains[:8]
    for at in range(8, gains.shape[0], 8):
        total = total + gains[at : at + 8]

    @pl.when(pl.program_id(0) == 0)
    def _():
        sum_ref[...] = jnp.zeros_like(sum_ref)

    sum_ref[...] += total


def norm_back_call(part, swapped, source, base, gain, rounded):
    rows, width = source.shape
    block = pl.BlockSpec((NORM_ROWS, width), lambda step: (step, 0))
    grad, total, *low = pl.pallas_call(
        norm_back_kernel,
        grid=(rows // NORM_ROWS,),
        in_specs=[block] * 4 + [pl.BlockSpec((1, width), lambda step: (0, 0))],
        out_specs=[block, pl.BlockSpec((8, width), lambda step: (0, 0))] + [block] * rounded,
        out_shape=[
            jax.ShapeDtypeStruct((rows, width), jnp.float32),
            jax.ShapeDtypeStruct((8, width), jnp.float32),
        ]
        + [jax.ShapeDtypeStruct((rows, width), jnp.bfloat16)] * rounded,
        cost_estimate=SMALL_COST,
        compiler_params=pltpu.CompilerParams(vmem_limit_bytes=VMEM_LIMIT),
        name="norm_back",
    )(part, swapped, source, base, gain[None, :])
    return (grad, jnp.sum(total, axis=0), *low)


def spread_kernel(query_ref, key_ref, value_ref, query_weight_ref, key_weight_ref, value_weight_ref, out_ref):
    def turned(ref):
        return ref[...].astype(jnp.float32).T.astype(jnp.bfloat16)

    out_ref[...] = (
        cols_dot(turned(query_ref), query_weight_ref[...])
        + cols_dot(turned(key_ref), key_weight_ref[...])
        + cols_dot(turned(value_ref), value_weight_ref[...])
    )


def spread_call(backs, weights):
    length = backs[0].shape[1]
    width = weights[0].shape[0]
    return pl.pallas_call(
        spread_kernel,
        grid=(length // BLOCK,),
        in_specs=[pl.BlockSpec((back.shape[0], BLOCK), lambda at: (0, at)) for back in backs]
        + [pl.BlockSpec(weight.shape, lambda at: (0, 0)) for weight in weights],
        out_specs=pl.BlockSpec((BLOCK, width), lambda at: (at, 0)),
        out_shape=jax.ShapeDtypeStruct((length, width), jnp.float32),
        cost_estimate=SMALL_COST,
        compiler_params=pltpu.CompilerParams(vmem_limit_bytes=VMEM_LIMIT),
        name="spread",
    )(*backs, *weights)


def far_kernel(count, *refs):
    parts, (factor_ref, select_ref, own_ref, low_ref, left_ref) = refs[:count], refs[count:]
    rows = own_ref.shape[1]

    @pl.when(pl.program_id(0) == 0)
    def _():
        start = 0
        for part in parts:
            size = part.shape[0]
            low_ref[start : start + size, :] = (part[...] * factor_ref[...]).astype(jnp.bfloat16)
            start += size

    left_ref[:, :rows] = own_ref[...]
    left_ref[:, rows:] = cols_dot(select_ref[...], low_ref[...]).astype(jnp.bfloat16)


def far_call(parts, factor, select, own):
    width, rows = own.shape
    step = 2 * BLOCK

    def whole(shape):
        return pl.BlockSpec(shape, lambda at: (0, 0))

    by_row = pl.BlockSpec((step, rows), lambda at: (at, 0))
    return pl.pallas_call(
        functools.partial(far_kernel, len(parts)),
        grid=(width // step,),
        in_specs=[whole(part.shape) for part in parts]
        + [whole(factor.shape), pl.BlockSpec((step, width), lambda at: (at, 0)), by_row],
        out_specs=[whole((rows, width)), pl.BlockSpec((step, 2 * rows), lambda at: (at, 0))],
        out_shape=[
            jax.ShapeDtypeStruct((rows, width), jnp.bfloat16),
            jax.ShapeDtypeStruct((width, 2 * rows), jnp.bfloat16),
        ],
        cost_estimate=SMALL_COST,
        compiler_params=pltpu.CompilerParams(vmem_limit_bytes=VMEM_LIMIT),
        name="far",
    )(*parts, factor, select, own)


def units_call(
    normed, incoming, gate_weight, up_weight, down_weight, first, count, sums, start=(), own=(), skip=0
):
    rows, width = normed.shape
    wide = 3 * BLOCK
    tile = wide if sums and count % wide == 0 and first % wide == 0 else BLOCK
    low = jnp.bfloat16
    whole = pl.BlockSpec((rows, width), lambda at, base: (0, 0), pipeline_mode=pl.Buffered(1))
    by_unit = pl.BlockSpec((width, tile), lambda at, base: (0, base[0] + at))
    own_tile = pl.BlockSpec((rows, tile), lambda at, base: (0, base[1] + at))
    out_rows = 2 * rows if own else rows
    out_tile = pl.BlockSpec((out_rows, tile), lambda at, base: (0, at))
    out_shape = [jax.ShapeDtypeStruct((out_rows, count), low)] * 3
    out_specs = [out_tile] * 3
    if sums:
        out_shape = out_shape + [jax.ShapeDtypeStruct((rows, width), jnp.float32)] * 2
        out_specs = out_specs + [pl.BlockSpec((rows, width), lambda at, base: (0, 0))] * 2
    base = jnp.stack([jnp.asarray(at // tile, jnp.int32) for at in (first, skip)])
    return pl.pallas_call(
        functools.partial(units_kernel, sums),
        grid_spec=pltpu.PrefetchScalarGridSpec(
            num_scalar_prefetch=1,
            grid=(count // tile,),
            in_specs=[
                whole,
                whole,
                by_unit,
                by_unit,
                pl.BlockSpec((tile, width), lambda at, base: (base[0] + at, 0)),
            ]
            + [whole] * len(start)
            + [own_tile] * len(own),
            out_specs=out_specs,
        ),
        out_shape=out_shape,
        compiler_params=pltpu.CompilerParams(vmem_limit_bytes=VMEM_LIMIT),
        cost_estimate=SMALL_COST,
        name="units",
    )(base, normed, incoming, gate_weight, up_weight, down_weight, *start, *own)


def contract_cols(left_side, right_side):
    return lax.dot_general(
        left_side, right_side, (((1,), (1,)), ((), ())), preferred_element_type=jnp.float32
    )


def contract_rows(left_side, right_side):
    return lax.dot_general(
        left_side, right_side, (((0,), (0,)), ((), ())), preferred_element_type=jnp.float32
    )


def product(left_side, right_side):
    return jnp.dot(left_side, right_side, preferred_element_type=jnp.float32)


def swap(value, axis):
    return lax.ppermute(value, axis, SWAP)


def core_sum(value):
    return value + swap(value, "tensor")


def core_sum_halves(make, rows):
    half = rows // 2
    first, second = make(0, half), make(half, rows)
    return jnp.concatenate([core_sum(first), core_sum(second)], axis=0)


def tie(*values):
    return lax.optimization_barrier(values)


class Line:
    def __init__(self, kept, length):
        own = kept.shape[0] // length
        self.blocks = [kept[at * own : (at + 1) * own] for at in range(length)]

    def go(self, aways):
        length = len(self.blocks)
        return {
            away: lax.ppermute(
                self.blocks[away], "line", [(at, (at + away) % length) for at in range(length)]
            )
            for away in aways
        }


def by_distance(*moved):
    together = {away: part for one in moved for away, part in one.items()}
    return [together[away] for away in sorted(together)]


def line_sum(own, arrived):
    for part in arrived:
        own = own + part
    return own


def pair_sums(own, arrived):
    mine, other = own, None
    for away, part in enumerate(arrived, 1):
        if away % 2 == 0:
            mine = mine + part
        else:
            other = part if other is None else other + part
    return mine, other


def in_order(half, mine, other):
    return jnp.concatenate(
        [jnp.where(half == 0, mine, other), jnp.where(half == 0, other, mine)], axis=1
    )


class Plane:
    def __init__(self, pieces):
        self.pieces = pieces

    def after(self, *values):
        lefts, values = tie([piece[0] for piece in self.pieces], values)
        self.pieces = [(left, *piece[1:]) for left, piece in zip(lefts, self.pieces)]
        return values

    @staticmethod
    def rows(left, start, stop):
        quarter = left.shape[0] // 4
        return left[start * quarter : stop * quarter]

    def products(self, for_near, for_mid):
        return [
            (contract_cols if transposed else product)(
                for_near(left) if near_first else for_mid(left), right
            )
            for left, right, near_first, transposed in self.pieces
        ]

    def send(self):
        return self.products(
            lambda left: self.rows(left, 0, 2), lambda left: self.rows(left, 1, 3)
        )

    def go(self, out):
        return [
            swap(part, "near" if piece[2] else "mid") for part, piece in zip(out, self.pieces)
        ]

    def halves(self, got):
        quarter = got[0].shape[0] // 2
        return [
            (late[quarter:], late[:quarter]) if piece[2] else (late[:quarter], late[quarter:])
            for late, piece in zip(got, self.pieces)
        ]

    def follow(self, got):
        parts = self.products(lambda left: self.rows(left, 2, 3), lambda left: self.rows(left, 0, 1))
        return [part + late for part, (late, _) in zip(parts, self.halves(got))]

    def pass_on(self, out):
        return [
            swap(part, "mid" if piece[2] else "near") for part, piece in zip(out, self.pieces)
        ]

    def hold(self, got):
        def own(left):
            return self.rows(left, 3, 4)

        parts = self.products(own, own)
        return [part + early for part, (_, early) in zip(parts, self.halves(got))]

    def keep(self, held, passed):
        return jnp.concatenate([part + late for part, late in zip(held, passed)], axis=1)


class Owners:
    def __init__(self, width):
        self.length = lax.axis_size("line")
        self.width = width
        self.own = width // (4 * self.length)
        line, mid, near = (lax.axis_index(name) for name in ("line", "mid", "near"))
        block = lax.broadcasted_iota(jnp.int32, (4, self.length, self.own, 1), 0)
        distance = lax.broadcasted_iota(jnp.int32, block.shape, 1)
        entry = lax.broadcasted_iota(jnp.int32, block.shape, 2)
        owner_near = (near + (block < 2)) % 2
        owner_mid = (mid + (block % 3 > 0)) % 2
        owner_line = (distance + line) % self.length
        feature = ((owner_line * 2 + owner_mid) * 2 + owner_near) * self.own + entry
        column = lax.broadcasted_iota(jnp.int32, (1, width), 1)
        (self.select,) = tie((feature.reshape(width, 1) == column).astype(jnp.bfloat16))

    def plane_first(self, left):
        return contract_cols(self.select, left).astype(jnp.bfloat16)


def in_line_order(found):
    length = len(found)
    stacked = jnp.stack(found)
    total = jnp.zeros_like(found[0])
    for at in range(length):
        away = (lax.axis_index("line") - at) % length
        total = total + lax.dynamic_index_in_dim(stacked, away, 0, keepdims=False)
    return total


def local(
    inputs,
    first_gain,
    query_weight,
    key_matrix,
    value_matrix,
    query_gain,
    key_gain,
    output_weight,
    second_gain,
    gate_weight,
    up_weight,
    down_weight,
    cotangent,
):
    row_count, model_width = inputs.shape
    head_dim = query_gain.shape[0]
    units = gate_weight.shape[1]
    cosine_table, sine_table = rope_tables(row_count, head_dim)
    owners = Owners(model_width)
    length = owners.length
    far_away = [length // 2]
    other_away = [away for away in range(1, length) if away != length // 2]

    core = lax.axis_index("tensor")
    half = lax.axis_index("line") % 2
    partners = [(at, at + 1 - 2 * (at % 2)) for at in range(length)]
    core_rows = row_count // 2

    def to_partner(value):
        return lax.ppermute(value, "line", partners)

    early = core_rows // 2

    def cotangent_part(start):
        part = lax.dynamic_slice_in_dim(cotangent, core * core_rows + start, early, axis=0)
        return part.astype(jnp.float32) * SHIFT

    far_first = to_partner(cotangent_part(0))
    normalized_input = rms_scale(inputs.astype(jnp.float32), first_gain).astype(jnp.bfloat16)

    def project(weight):
        return lax.dot_general(
            weight,
            normalized_input,
            (((0,), (1,)), ((), ())),
            preferred_element_type=jnp.float32,
        )

    query_proj, projected_key = project(query_weight), project(key_matrix)
    gains = (query_gain[:, None], key_gain[:, None])
    kept = attend(
        query_proj, projected_key, project(value_matrix), *gains, cosine_table, sine_table
    )
    *kept, far_first, cotangent = tie(*kept, far_first, cotangent)
    mixed = kept[0]
    far_second = to_partner(cotangent_part(early))
    attention = [
        contract_rows(mixed[:, at : at + core_rows], output_weight)
        for at in range(0, row_count, core_rows)
    ]
    middle, hat, normed_mid = norm_call(
        [(part, swap(part, "tensor")) for part in attention], inputs, second_gain, core
    )
    hat, normed_mid = tie(hat, normed_mid)
    hat_far = to_partner(hat)

    weights = (gate_weight, up_weight, down_weight)

    alone = units // 3 // 256 * 256
    paired = (units - alone) // 2
    hidden_1, gate_1, up_1, *sums_1 = units_call(normed_mid, cotangent, *weights, 0, alone, 1)
    normed_left = owners.plane_first(normed_mid)
    cotangent_left = owners.plane_first(cotangent)
    plane_1 = Plane(
        [(cotangent_left, hidden_1, True, False), (normed_left, gate_1, False, False)]
    )
    sent_1 = plane_1.send()
    far = [far_first, far_second]
    sent_1, normed_mid, far, normed_left = tie(sent_1, normed_mid, far, normed_left)
    got_1 = plane_1.go(sent_1)
    far = far + [swap(part, "tensor") for part in far]
    hidden_2, gate_2, up_2, mid_part, branch_part = units_call(
        normed_mid, cotangent, *weights, alone, units - alone, 2, sums_1
    )
    got_1, mid_part, hat_far, far, up_1, normed_left = tie(
        got_1, mid_part, hat_far, far, up_1, normed_left
    )
    up_cut = alone // 256 * 128
    plane_u = Plane(
        [(normed_left, up_1[:, :up_cut], True, False), (normed_left, up_1[:, up_cut:], False, False)]
    )
    sent_u = plane_u.send()
    sent_u, got_1, hat_far, far = tie(sent_u, got_1, hat_far, far)

    got_u = plane_u.go(sent_u)
    hat_swapped = swap(hat_far, "tensor")
    follow_1 = plane_1.follow(got_1)
    far_cotangent, cotangent_both = far_call(
        far, jnp.full((1, model_width), 1.0 / SHIFT, jnp.float32), owners.select, cotangent_left
    )
    far_normed, normed_both = far_call(
        [hat_far, hat_swapped], second_gain[None, :], owners.select, normed_left
    )
    got_u, follow_1, far_normed, normed_both, far_cotangent, mid_part = tie(
        got_u, follow_1, far_normed, normed_both, far_cotangent, mid_part
    )
    passed_1 = plane_1.pass_on(follow_1)
    mid_swapped = swap(mid_part, "tensor")
    hidden_both, gate_both, up_both = units_call(
        far_normed,
        far_cotangent,
        *weights,
        alone + half * paired,
        paired,
        0,
        own=(hidden_2, gate_2, up_2),
        skip=half * paired,
    )
    passed_1, normed_both, hidden_both, gate_both, up_both, mid_swapped = tie(
        passed_1, normed_both, hidden_both, gate_both, up_both, mid_swapped
    )
    follow_u = plane_u.follow(got_u)
    follow_u, normed_both, hidden_both, gate_both, passed_1 = tie(
        follow_u, normed_both, hidden_both, gate_both, passed_1
    )
    passed_u = plane_u.pass_on(follow_u)
    plane_2 = Plane(
        [(cotangent_both, hidden_both, True, False), (normed_both, gate_both, False, False)]
    )
    sent_2 = plane_2.send()
    sent_2, passed_1, passed_u, mid_swapped, up_both, normalized_input = plane_u.after(
        *plane_1.after(sent_2, passed_1, passed_u, mid_swapped, up_both, normalized_input)
    )
    got_2 = plane_2.go(sent_2)
    line_1 = Line(
        jnp.concatenate([plane_1.keep(plane_1.hold(got_1), passed_1), plane_u.keep(plane_u.hold(got_u), passed_u)], axis=1),
        length,
    )
    moved_1 = line_1.go(other_away)
    middle_grad, second_gain_grad, attention_back = norm_back_call(
        mid_part, mid_swapped, middle, cotangent, second_gain, True
    )
    mixed_back = contract_cols(output_weight, attention_back).astype(jnp.bfloat16)
    up_cut = paired * 5 // 6 // 128 * 128
    plane_3 = Plane(
        [
            (normed_both, up_both[:, :up_cut], True, False),
            (normed_both, up_both[:, up_cut:], False, False),
            (owners.plane_first(attention_back), mixed, False, True),
        ]
    )
    sent_3 = plane_3.send()
    branch_swapped = swap(branch_part, "tensor")
    got_2, moved_1, mixed_back, sent_3, normalized_input, branch_swapped = tie(
        got_2, moved_1, mixed_back, sent_3, normalized_input, branch_swapped
    )
    follow_2 = plane_2.follow(got_2)
    follow_2, mixed_back, branch_part = tie(follow_2, mixed_back, branch_part)
    passed_2 = plane_2.pass_on(follow_2)
    later_1 = line_1.go(far_away)
    query_back, key_back, value_back, query_part, key_part = attend_back(
        query_proj, projected_key, *gains, cosine_table, sine_table, kept, mixed_back
    )
    normed_part = spread_call(
        (query_back, key_back, value_back), (query_weight, key_matrix, value_matrix)
    )
    passed_2, moved_1, later_1, sent_3, query_back, key_back, value_back, normalized_input = (
        plane_2.after(
            passed_2, moved_1, later_1, sent_3, query_back, key_back, value_back, normalized_input
        )
    )
    got_3 = plane_3.go(sent_3)
    line_2 = Line(plane_2.keep(plane_2.hold(got_2), passed_2), length)
    moved_2 = line_2.go(other_away)
    got_3, moved_2, normed_part, branch_part, branch_swapped = tie(
        got_3, moved_2, normed_part, branch_part, branch_swapped
    )
    follow_3 = plane_3.follow(got_3)
    head_gains = core_sum(
        jnp.concatenate(
            [
                jnp.sum(part.reshape(-1, head_dim, 128), axis=(0, 2))
                for part in (query_part, key_part)
            ]
        )
    )
    follow_3, normed_part, head_gains, normalized_input = tie(
        follow_3, normed_part, head_gains, normalized_input
    )
    passed_3 = plane_3.pass_on(follow_3)
    later_2 = line_2.go(far_away)
    input_left = owners.plane_first(normalized_input)
    plane_4 = Plane(
        [
            (input_left, jnp.concatenate([key_back, value_back], axis=0), True, True),
            (input_left, query_back, False, True),
        ]
    )
    sent_4 = plane_4.send()
    input_grad, first_gain_grad = norm_back_call(
        normed_part, swap(normed_part, "tensor"), inputs, middle_grad, first_gain, False
    )
    rows = jnp.stack(
        [
            first_gain_grad,
            second_gain_grad,
            jnp.pad(head_gains, (0, model_width - 2 * head_dim)),
        ]
    )
    rows = jnp.pad(rows, ((0, 5), (0, 0)))
    passed_3, moved_1, later_1, moved_2, later_2, sent_4, input_grad, rows, branch_part = (
        plane_3.after(
            passed_3, moved_1, later_1, moved_2, later_2, sent_4, input_grad, rows, branch_part
        )
    )
    got_4 = plane_4.go(sent_4)
    line_3 = Line(plane_3.keep(plane_3.hold(got_3), passed_3), length)
    moved_3 = line_3.go(other_away)
    rows = rows + swap(rows, "near")
    got_4, moved_3, rows, branch_part = tie(got_4, moved_3, rows, branch_part)
    follow_4 = plane_4.follow(got_4)
    follow_4, rows = tie(follow_4, rows)
    passed_4 = plane_4.pass_on(follow_4)
    held_4 = plane_4.hold(got_4)
    later_3 = line_3.go(far_away)
    rows = rows + swap(rows, "mid")
    held_4, passed_4, moved_1, later_1, moved_2, later_2, moved_3, later_3, rows, branch_part = tie(
        held_4, passed_4, moved_1, later_1, moved_2, later_2, moved_3, later_3, rows, branch_part
    )
    line_4 = Line(plane_4.keep(held_4, passed_4), length)
    kept_rows = line_4.blocks[0].shape[0]
    line_4.blocks = [jnp.concatenate([block, rows], axis=0) for block in line_4.blocks]
    moved_4 = line_4.go(far_away + other_away)
    moved_4[far_away[0]], branch_part, moved_1, later_1, moved_2, later_2, moved_3, later_3 = tie(
        moved_4[far_away[0]], branch_part, moved_1, later_1, moved_2, later_2, moved_3, later_3
    )
    moved_4 = by_distance(moved_4)
    result = (middle + (branch_part + branch_swapped)).astype(jnp.bfloat16)
    rows = in_line_order([rows] + [part[kept_rows:] for part in moved_4])
    attention_shard = line_sum(
        line_4.blocks[0][:kept_rows], [part[:kept_rows] for part in moved_4]
    )

    def split(total, count):
        return [total[:, at : at + count] for at in range(0, total.shape[1], count)]

    halves = [split(side, paired) for side in pair_sums(line_2.blocks[0], by_distance(moved_2, later_2))]
    moved_3 = by_distance(moved_3, later_3)
    sides = [side[:, :paired] for side in pair_sums(line_3.blocks[0], moved_3)]
    down_2, gate_2, up_2 = (
        in_order(half, mine, other)
        for mine, other in zip(halves[0] + sides[:1], halves[1] + sides[1:])
    )
    first = line_sum(line_1.blocks[0], by_distance(moved_1, later_1))
    down_1, gate_1, up_1 = split(first, alone)
    down_shard, gate_shard, up_shard = (
        jnp.concatenate(pair, axis=1)
        for pair in ((down_1, down_2), (gate_1, gate_2), (up_1, up_2))
    )
    output_shard = line_sum(
        line_3.blocks[0][:, paired:], [part[:, paired:] for part in moved_3]
    )
    key_cut = key_back.shape[0]
    pair_cut = 2 * key_cut
    index = (lax.axis_index("line") * 2 + lax.axis_index("mid")) * 2 + lax.axis_index("near")
    gains = lax.dynamic_slice(rows, (0, index * owners.own), (2, owners.own))
    return (
        result,
        input_grad,
        gains[0],
        attention_shard[:, pair_cut:],
        attention_shard[:, :key_cut],
        attention_shard[:, key_cut:pair_cut],
        rows[2, :head_dim],
        rows[2, head_dim : 2 * head_dim],
        output_shard.T,
        gains[1],
        gate_shard,
        up_shard,
        down_shard.T,
    )


def solution(mesh):
    line = mesh.shape["dp"] // 4
    shaped = Mesh(
        mesh.devices.reshape(line, 2, 2, mesh.shape["tensor"]), ("line", "mid", "near", "tensor")
    )
    dp = ("line", "mid", "near")
    placed = (
        P(dp, None),
        P(),
        P(None, "tensor"),
        P(None, "tensor"),
        P(None, "tensor"),
        P(),
        P(),
        P("tensor", None),
        P(),
        P(None, "tensor"),
        P(None, "tensor"),
        P("tensor", None),
        P(dp, None),
    )
    return jax.shard_map(
        local,
        mesh=shaped,
        in_specs=placed,
        out_specs=(
            P(dp, None),
            P(dp, None),
            P(dp),
            P(dp, "tensor"),
            P(dp, "tensor"),
            P(dp, "tensor"),
            P(),
            P(),
            P("tensor", dp),
            P(dp),
            P(dp, "tensor"),
            P(dp, "tensor"),
            P("tensor", dp),
        ),
        check_vma=False,
    )
```
